32 devices in a mesh: dp: 8 (over z, x), tensor: 4 (over y, core).
Axes of the slice: x: 2, y: 2, z: 4, core: 2. Of those that a mesh axis runs over, the one named last changes fastest.
Arguments:
- latents: bfloat16 [1024, 16, 1024], P('tensor', 'dp'), may hold values from -6 to 6
- conditioning: bfloat16 [16, 1024], P('dp'), may hold values from -6 to 6
- mod_weight: bfloat16 [1024, 6, 1024], P('dp'), may hold values from -0.1875 to 0.1875
- mod_bias: bfloat16 [6, 1024], replicated, may hold values from -3 to 3
- qkv_weight: bfloat16 [1024, 3, 1024], P('dp', None, 'tensor'), may hold values from -0.1875 to 0.1875
- qkv_bias: bfloat16 [3, 1024], P(None, 'tensor'), may hold values from -2 to 2
- proj_weight: bfloat16 [1024, 1024], P('dp', 'tensor'), may hold values from -0.75 to 0.75
- proj_bias: bfloat16 [1024], replicated, may hold values from -2 to 2
- expand_weight: bfloat16 [1024, 4096], P('dp', 'tensor'), may hold values from -0.1875 to 0.1875
- expand_bias: bfloat16 [4096], P('tensor'), may hold values from -2 to 2
- reduce_weight: bfloat16 [1024, 4096], P('dp', 'tensor'), may hold values from -0.125 to 0.125
- reduce_bias: bfloat16 [1024], replicated, may hold values from -2 to 2
- out_grad: bfloat16 [1024, 16, 1024], P('tensor', 'dp'), may hold values from -6 to 6
Outputs:
- layer_out: bfloat16 [1024, 16, 1024], P('tensor', 'dp')
- latent_grad: float32 [1024, 16, 1024], P('tensor', 'dp')
- cond_grad: float32 [16, 1024], P('dp')
- mod_weight_grad: float32 [1024, 6, 1024], P('dp', None, 'tensor')
- mod_bias_grad: float32 [6, 1024], replicated
- qkv_weight_grad: float32 [1024, 3, 1024], P('dp', None, 'tensor')
- qkv_bias_grad: float32 [3, 1024], P(None, 'tensor')
- proj_weight_grad: float32 [1024, 1024], P('dp', 'tensor')
- proj_bias_grad: float32 [1024], replicated
- expand_weight_grad: float32 [1024, 4096], P('dp', 'tensor')
- expand_bias_grad: float32 [4096], P('tensor')
- reduce_weight_grad: float32 [1024, 4096], P('dp', 'tensor')
- reduce_bias_grad: float32 [1024], replicated
The draws below stay inside these ranges and needn't reach their ends.
All inputs are finite; a program needn't handle non-finite values.
Results may differ from the reference program's by a relative error of at most 0.02.
The reference program's roundings to bfloat16 on the way count: a program that leaves them out, or rounds other values in their place, can miss the bound.
Values may be sent and summed in bfloat16 or wider, within the bound.
No kernel may reach another device: no remote copies, remote signals or barrier semaphores. Data moves between devices by JAX's collectives and lax.ppermute only.
A program may use at most 256 MiB of HBM per device.

```python
import jax
import jax.numpy as jnp
from jax import lax

D = 1024
HEADS = 16
HEAD_DIM = 64
FF = 4096
SEQ = 1024
IMAGES = 16


def levels(key, dims, pieces, smallest, high):
    def one(dim, parts):
        steps = jax.random.uniform(jax.random.fold_in(jax.random.fold_in(key, 6), dim), (parts,), jnp.float32, smallest / len(pieces), high / len(pieces))
        return jnp.repeat(jnp.exp(steps), dims[dim] // parts).reshape((-1,) + (1,) * (len(dims) - dim - 1))

    loudness = one(*pieces[0])
    for cut in pieces[1:]:
        loudness = loudness * one(*cut)
    return loudness


def noise(key, extent, width, bound, pieces=(), held_as=jnp.bfloat16):
    level = levels(key, extent, pieces, -0.22, 0.18) if pieces else 1.0
    result = jax.random.normal(key, extent, jnp.float32) * width * level
    return jnp.minimum(jnp.maximum(result, -bound), bound).astype(held_as)


def setup_inputs(seed: int = 0) -> dict:
    keys = jax.random.split(jax.random.key(seed), 14)
    return {
        "latents": noise(keys[0], (SEQ, IMAGES, D), 1.0, 6.0, ((0, 4), (1, 8))),
        "conditioning": noise(keys[1], (IMAGES, D), 1.0, 6.0, ((0, 8),)),
        "mod_weight": noise(keys[2], (D, 6, D), D ** -0.5, 0.1875, ((0, 8),)),
        "mod_bias": noise(keys[3], (6, D), 0.5, 3.0),
        "qkv_weight": noise(keys[4], (D, 3, D), D ** -0.5, 0.1875, ((0, 8), (2, 4))),
        "qkv_bias": noise(keys[5], (3, D), 0.3, 2.0, ((1, 4),)),
        "proj_weight": noise(keys[6], (D, D), (D // 16) ** -0.5, 0.75, ((0, 8), (1, 4))),
        "proj_bias": noise(keys[7], (D,), 0.3, 2.0),
        "expand_weight": noise(keys[8], (D, FF), D ** -0.5, 0.1875, ((0, 8), (1, 4))),
        "expand_bias": noise(keys[9], (FF,), 0.3, 2.0, ((0, 4),)),
        "reduce_weight": noise(keys[10], (D, FF), (FF // 2) ** -0.5, 0.125, ((0, 8), (1, 4))),
        "reduce_bias": noise(keys[11], (D,), 0.3, 2.0),
        "out_grad": noise(keys[12], (SEQ, IMAGES, D), 1.0, 6.0, ((0, 4), (1, 8))),
    }


@jax.custom_vjp
def low(v):
    return lax.optimization_barrier(v.astype(jnp.bfloat16)).astype(jnp.float32)

@jax.custom_vjp
def low_back(v):
    return v

def low_keep(v):
    return (low(v), None)

def low_pass(kept, grad):
    return (grad,)

def back_keep(v):
    return (v, None)

def back_low(kept, grad):
    return (low(grad),)
low.defvjp(low_keep, low_pass)
low_back.defvjp(back_keep, back_low)

def product(form, left, right):
    return jnp.einsum(form, left, right, precision=lax.Precision.HIGHEST)

def norm_rows(values):
    mean_val = lax.optimization_barrier(jnp.mean(values, -1, keepdims=True))
    centered = values - mean_val
    variance = lax.optimization_barrier(jnp.mean(centered * centered, -1, keepdims=True))
    return centered * lax.rsqrt(variance + 1e-06)

def attend_block(query_part, key_all, value_all):
    scores = low_back(product('qghe,kghe->ghqk', query_part, key_all) * HEAD_DIM ** (-0.5))
    probs = low(jax.nn.softmax(scores, axis=-1))
    return product('ghqk,kghe->qghe', probs, value_all)

def forward(latent_in, cond_in, mod_weight, mod_bias, qkv_weight, qkv_bias, proj_weight, proj_bias, expand_weight, expand_bias, reduce_weight, reduce_bias):
    seq_len = latent_in.shape[0]
    images = latent_in.shape[1]
    cond_act = low(jax.nn.silu(cond_in))
    modulation = low_back(product('gd,dke->gke', cond_act, mod_weight)) + mod_bias
    shifted_a = low(norm_rows(latent_in) * (1.0 + modulation[:, 1]) + modulation[:, 0])
    qkv_all = low_back(low(product('sgd,dke->sgke', shifted_a, qkv_weight) + qkv_bias))
    query = qkv_all[:, :, 0].reshape(seq_len, images, HEADS, HEAD_DIM)
    key_all = qkv_all[:, :, 1].reshape(seq_len, images, HEADS, HEAD_DIM)
    value_all = qkv_all[:, :, 2].reshape(seq_len, images, HEADS, HEAD_DIM)
    query_block = min(512, seq_len)
    blocks = query.reshape(seq_len // query_block, query_block, images, HEADS, HEAD_DIM)
    attended = lax.map(lambda part_q: jax.checkpoint(attend_block)(part_q, key_all, value_all), blocks)
    attended = low_back(low(attended.reshape(seq_len, images, D)))
    branch_a = low_back(product('sge,oe->sgo', attended, proj_weight) + proj_bias)
    mid_resid = latent_in + modulation[:, 2] * branch_a
    shifted_m = low(norm_rows(mid_resid) * (1.0 + modulation[:, 4]) + modulation[:, 3])
    pre_act = low_back(product('sgd,df->sgf', shifted_m, expand_weight) + expand_bias)
    hidden = low(jax.nn.gelu(pre_act, approximate=True))
    branch_m = low_back(product('sgf,of->sgo', hidden, reduce_weight) + reduce_bias)
    return mid_resid + modulation[:, 5] * branch_m

def reference(latents, conditioning, mod_weight, mod_bias, qkv_weight, qkv_bias, proj_weight, proj_bias, expand_weight, expand_bias, reduce_weight, reduce_bias, out_grad):
    group_size = 4
    groups = IMAGES // group_size
    params = tuple((param.astype(jnp.float32) for param in (mod_weight, mod_bias, qkv_weight, qkv_bias, proj_weight, proj_bias, expand_weight, expand_bias, reduce_weight, reduce_bias)))
    latent_groups = latents.astype(jnp.float32).reshape(SEQ, groups, group_size, D).transpose(1, 0, 2, 3)
    cond_groups = conditioning.astype(jnp.float32).reshape(groups, group_size, D)
    cot_groups = out_grad.astype(jnp.float32).reshape(SEQ, groups, group_size, D).transpose(1, 0, 2, 3)

    def step(running, group_in):
        latent_g, cond_g, cot_g = group_in
        layer_val, pull_back = jax.vjp(forward, latent_g, cond_g, *params)
        grads = pull_back(cot_g)
        running = tuple((total + grad for total, grad in zip(running, grads[2:])))
        return (running, (layer_val, grads[0], grads[1]))
    init = tuple((jnp.zeros_like(param) for param in params))
    totals, (values, latent_grads, cond_grads) = lax.scan(step, init, (latent_groups, cond_groups, cot_groups))
    layer_out = values.transpose(1, 0, 2, 3).reshape(SEQ, IMAGES, D).astype(jnp.bfloat16)
    latent_grad = latent_grads.transpose(1, 0, 2, 3).reshape(SEQ, IMAGES, D)
    cond_grad = cond_grads.reshape(IMAGES, D)
    return (layer_out, latent_grad, cond_grad, totals[0], totals[1], totals[2], totals[3], totals[4], totals[5], totals[6], totals[7], totals[8], totals[9])
```

```python
import functools

import jax
import jax.numpy as jnp
from jax import lax
from jax.experimental import pallas as pl
from jax.experimental.pallas import tpu as pltpu
from jax.sharding import PartitionSpec as P

HEAD_DIM = 64
F32 = jnp.float32
BF16 = jnp.bfloat16
LOG2E = 1.4426950408889634
GELU_C = 0.7978845608028654
GELU_A = 0.044715
NN = (((1,), (0,)), ((), ()))
NT = (((1,), (1,)), ((), ()))
VMEM_BYTES = 56 * 1024 * 1024


def dot(left, right, dims=NN):
    return lax.dot_general(left, right, dims, preferred_element_type=F32)


def params(*kinds):
    return pltpu.CompilerParams(dimension_semantics=kinds, vmem_limit_bytes=VMEM_BYTES)


def attend_kernel(chunk, q_ref, k_ref, v_ref, out_ref, lse_ref):
    length, width = q_ref.shape
    factor = HEAD_DIM ** (-0.5) * LOG2E
    values_t = v_ref[...].astype(F32).T.astype(BF16)
    keys = [k_ref[:, lo : lo + HEAD_DIM] for lo in range(0, width, HEAD_DIM)]

    def body(step, carry):
        rows = pl.ds(pl.multiple_of(step * chunk, chunk), chunk)
        outs = []
        for head, key in enumerate(keys):
            lo = head * HEAD_DIM
            scores = dot(key, q_ref[rows, lo : lo + HEAD_DIM], NT)
            top = jnp.max(scores, 0, keepdims=True)
            weights = jnp.exp2((scores - top) * factor)
            total = jnp.sum(weights, 0, keepdims=True)
            out_t = dot(values_t[lo : lo + HEAD_DIM], weights.astype(BF16))
            outs.append(out_t / total)
            lse_ref[0, head : head + 1, rows] = top * factor + jnp.log(total) * LOG2E
        out_ref[rows, :] = jnp.concatenate(outs, 0).T.astype(BF16)
        return carry

    lax.fori_loop(0, length // chunk, body, 0)


def attend(qkv):
    length, three = qkv.shape
    width = three // 3
    pairs = width // 128
    chunk = min(256, length)
    flops = 4 * length * length * width
    spec = lambda part: pl.BlockSpec((length, 128), lambda i: (0, part * pairs + i))
    return pl.pallas_call(
        functools.partial(attend_kernel, chunk),
        grid=(pairs,),
        in_specs=[spec(0), spec(1), spec(2)],
        out_specs=[
            pl.BlockSpec((length, 128), lambda i: (0, i)),
            pl.BlockSpec((1, 8, length), lambda i: (i, 0, 0)),
        ],
        out_shape=[
            jax.ShapeDtypeStruct((length, width), BF16),
            jax.ShapeDtypeStruct((pairs, 8, length), F32),
        ],
        compiler_params=params("arbitrary"),
        cost_estimate=pl.CostEstimate(
            flops=4 * flops, bytes_accessed=8 * length * width, transcendentals=length * length
        ),
        name="attend",
    )(qkv, qkv, qkv)


def attend_back_kernel(chunk, q_ref, k_ref, v_ref, g_ref, lse_ref, out_ref, dk_ref, dv_ref):
    length, width = q_ref.shape
    total_width = out_ref.shape[1] // 3
    scale = HEAD_DIM ** (-0.5)
    factor = scale * LOG2E
    pair = pl.program_id(0)
    keys_t = k_ref[...].astype(F32).T.astype(BF16)
    heads = range(0, width, HEAD_DIM)
    keys = [k_ref[:, lo : lo + HEAD_DIM] for lo in heads]
    values = [v_ref[:, lo : lo + HEAD_DIM] for lo in heads]
    dk_ref[...] = jnp.zeros_like(dk_ref)
    dv_ref[...] = jnp.zeros_like(dv_ref)

    def columns(part):
        return pl.ds(pl.multiple_of(part * total_width + pair * width, width), width)

    def body(step, carry):
        rows = pl.ds(pl.multiple_of(step * chunk, chunk), chunk)
        outs = []
        for head, (key, value) in enumerate(zip(keys, values)):
            lo = head * HEAD_DIM
            query = q_ref[rows, lo : lo + HEAD_DIM]
            grad = g_ref[rows, lo : lo + HEAD_DIM]
            probs = jnp.exp2(dot(key, query, NT) * factor - lse_ref[0, head : head + 1, rows])
            dv_ref[head] += dot(probs.astype(BF16), grad)
            weighted = probs * dot(value, grad, NT)
            row_dot = jnp.sum(weighted, 0, keepdims=True)
            g_scores = (weighted - probs * row_dot).astype(BF16)
            dk_ref[head] += dot(g_scores, query)
            outs.append(dot(keys_t[lo : lo + HEAD_DIM], g_scores) * scale)
        out_ref[rows, columns(0)] = jnp.concatenate(outs, 0).T.astype(BF16)
        return carry

    lax.fori_loop(0, length // chunk, body, 0)
    n_heads = len(keys)
    out_ref[:, columns(1)] = (
        jnp.concatenate([dk_ref[h] for h in range(n_heads)], 1) * scale
    ).astype(BF16)
    out_ref[:, columns(2)] = jnp.concatenate([dv_ref[h] for h in range(n_heads)], 1).astype(BF16)


def attend_back(qkv, grad_att, lse):
    length, three = qkv.shape
    width = three // 3
    pairs = width // 128
    chunk = min(256, length)
    flops = 10 * length * length * width
    spec = lambda part: pl.BlockSpec((length, 128), lambda i: (0, part * pairs + i))
    return pl.pallas_call(
        functools.partial(attend_back_kernel, chunk),
        grid=(pairs,),
        in_specs=[
            spec(0),
            spec(1),
            spec(2),
            pl.BlockSpec((length, 128), lambda i: (0, i)),
            pl.BlockSpec((1, 8, length), lambda i: (i, 0, 0)),
        ],
        out_specs=pl.BlockSpec((length, three), lambda i: (0, 0)),
        out_shape=jax.ShapeDtypeStruct((length, three), BF16),
        scratch_shapes=[
            pltpu.VMEM((128 // HEAD_DIM, length, HEAD_DIM), F32),
            pltpu.VMEM((128 // HEAD_DIM, length, HEAD_DIM), F32),
        ],
        compiler_params=params("arbitrary"),
        cost_estimate=pl.CostEstimate(
            flops=4 * flops, bytes_accessed=16 * length * width, transcendentals=length * length
        ),
        name="attend_back",
    )(qkv, qkv, qkv, grad_att, lse)


def mlp_kernel(
    x_ref, g_ref, up_ref, down_ref, bias_ref, hid_ref, gpre_ref, out_ref, gx_ref, gbias_ref
):
    pre = dot(x_ref[...], up_ref[...]) + bias_ref[...].astype(F32)
    square = pre * pre
    th = jnp.tanh(GELU_C * pre * (1.0 + GELU_A * square))
    half = 0.5 * (1.0 + th)
    hidden = (pre * half).astype(BF16)
    slope = half + (0.5 * GELU_C) * pre * (1.0 - th * th) * (1.0 + 3.0 * GELU_A * square)
    g_pre = (dot(g_ref[...], down_ref[...]) * slope).astype(BF16)
    hid_ref[...] = hidden
    gpre_ref[...] = g_pre
    gx_ref[...] = dot(g_pre, up_ref[...], NT).astype(BF16)
    out_ref[...] = dot(hidden, down_ref[...], NT).astype(BF16)

    @pl.when(pl.program_id(0) == 0)
    def _():
        gbias_ref[...] = jnp.zeros_like(gbias_ref)

    gbias_ref[...] += jnp.sum(g_pre.astype(F32), 0, keepdims=True)


def mlp(x_full, g_full, up, down, bias):
    tokens, width = x_full.shape
    hidden = up.shape[1]
    tile = min(256, tokens)
    rows = lambda cols: pl.BlockSpec((tile, cols), lambda i: (i, 0))
    whole = lambda r, c: pl.BlockSpec((r, c), lambda i: (0, 0))
    return pl.pallas_call(
        mlp_kernel,
        grid=(tokens // tile,),
        in_specs=[
            rows(width),
            rows(width),
            whole(width, hidden),
            whole(width, hidden),
            whole(1, hidden),
        ],
        out_specs=[rows(hidden), rows(hidden), rows(width), rows(width), whole(1, hidden)],
        out_shape=[
            jax.ShapeDtypeStruct((tokens, hidden), BF16),
            jax.ShapeDtypeStruct((tokens, hidden), BF16),
            jax.ShapeDtypeStruct((tokens, width), BF16),
            jax.ShapeDtypeStruct((tokens, width), BF16),
            jax.ShapeDtypeStruct((1, hidden), F32),
        ],
        compiler_params=params("arbitrary"),
        cost_estimate=pl.CostEstimate(
            flops=8 * tokens * width * hidden,
            bytes_accessed=12 * tokens * width + 4 * width * hidden,
            transcendentals=tokens * hidden,
        ),
        name="feed_forward",
    )(x_full, g_full, up, down, bias)


def norm_parts(values):
    centered = values - jnp.mean(values, -1, keepdims=True)
    scale = lax.rsqrt(jnp.mean(centered * centered, -1, keepdims=True) + 1e-06)
    return centered * scale, scale


def norm_back(normed, scale, grad):
    mean_g = jnp.mean(grad, -1, keepdims=True)
    mean_gn = jnp.mean(grad * normed, -1, keepdims=True)
    return scale * (grad - mean_g - normed * mean_gn)


def swap(value, bit):
    n = lax.axis_size("tensor")
    return lax.ppermute(value, "tensor", [(i, i ^ bit) for i in range(n)])


def spread(value):
    pair = jnp.concatenate([value, swap(value, 2)], 0)
    return jnp.concatenate([pair, swap(pair, 1)], 0)


def collect(value):
    half = value.shape[0] // 2
    pair = value[:half].astype(F32) + swap(value[half:], 1).astype(F32)
    own = half // 2
    return pair[:own] + swap(pair[own:].astype(BF16), 2).astype(F32)


def per_device(
    latents,
    conditioning,
    mod_weight,
    mod_bias,
    qkv_weight,
    qkv_bias,
    proj_weight,
    proj_bias,
    expand_weight,
    expand_bias,
    reduce_weight,
    reduce_bias,
    out_grad,
):
    n_tensor = lax.axis_size("tensor")
    n_dp = lax.axis_size("dp")
    row_count, images, model_width = latents.shape
    local_width = qkv_weight.shape[2]
    hidden_width = expand_weight.shape[1]
    mod_rows = mod_weight.shape[0]

    qkv_full = lax.all_gather(
        qkv_weight.reshape(mod_rows, 3 * local_width), "dp", axis=0, tiled=True
    )
    rest = jnp.concatenate([expand_weight, reduce_weight, proj_weight], 1)
    rest, qkv_full = lax.optimization_barrier((rest, qkv_full))
    rest_full = lax.all_gather(rest, "dp", axis=0, tiled=True)
    expand_full = rest_full[:, :hidden_width]
    reduce_full = rest_full[:, hidden_width : 2 * hidden_width]
    proj_full = rest_full[:, 2 * hidden_width :]

    cond_float = conditioning.astype(F32)
    cond_low = jax.nn.silu(cond_float).astype(BF16)
    cond_cols = lax.all_to_all(
        cond_low.reshape(images, n_dp, mod_rows).transpose(1, 0, 2), "dp", 0, 0, tiled=True
    ).reshape(n_dp * images, mod_rows)
    mod_part = jnp.einsum("gd,dke->gke", cond_cols, mod_weight, preferred_element_type=F32)
    mod_sum = jnp.sum(
        lax.all_to_all(
            mod_part.reshape(n_dp, images, 6, model_width), "dp", 0, 0, tiled=True
        ).reshape(n_dp, images, 6, model_width),
        0,
    )
    modulation = mod_sum + mod_bias.astype(F32)[None]

    x = [latents[:, i].astype(F32) for i in range(images)]
    grad_y = [out_grad[:, i].astype(F32) for i in range(images)]
    mod = [[modulation[i, k] for k in range(6)] for i in range(images)]
    both = range(images)

    norm_a = [norm_parts(x[i]) for i in both]
    shifted_a = [(norm_a[i][0] * (1.0 + mod[i][1]) + mod[i][0]).astype(BF16) for i in both]
    full_a = [spread(v) for v in shifted_a]
    grad_m = [(grad_y[i] * mod[i][5]).astype(BF16) for i in both]
    full_gm = [spread(v) for v in grad_m]

    bias_qkv = qkv_bias.astype(F32).reshape(1, 3 * local_width)
    qkv = [(dot(v, qkv_full) + bias_qkv).astype(BF16) for v in full_a]
    attended = [attend(v) for v in qkv]
    branch_a = [
        collect(dot(out, proj_full, NT).astype(BF16)) + proj_bias.astype(F32)
        for out, _ in attended
    ]
    mid = [x[i] + mod[i][2] * branch_a[i] for i in both]
    norm_m = [norm_parts(mid[i]) for i in both]
    shifted_m = [(norm_m[i][0] * (1.0 + mod[i][4]) + mod[i][3]).astype(BF16) for i in both]
    full_m = [spread(v) for v in shifted_m]

    ff = [
        mlp(full_m[i], full_gm[i], expand_full, reduce_full, expand_bias.reshape(1, hidden_width))
        for i in both
    ]
    grad_sm = [collect(ff[i][3]) for i in both]
    branch_m = [collect(ff[i][2]) + reduce_bias.astype(F32) for i in both]
    result = jnp.stack([(mid[i] + mod[i][5] * branch_m[i]).astype(BF16) for i in both], 1)

    tn = (((0,), (0,)), ((), ()))

    def weight_grad(lefts, rights):
        total = dot(lefts[0], rights[0], tn)
        for left, right in zip(lefts[1:], rights[1:]):
            total = total + dot(left, right, tn)
        return total.astype(BF16)

    def scatter_rows(value):
        return lax.psum_scatter(value, "dp", scatter_dimension=0, tiled=True).astype(F32)

    g_reduce_w = scatter_rows(weight_grad(full_gm, [f[0] for f in ff]))
    g_expand_w = scatter_rows(weight_grad(full_m, [f[1] for f in ff]))

    grad_mid = [
        grad_y[i] + norm_back(*norm_m[i], grad_sm[i] * (1.0 + mod[i][4])) for i in both
    ]
    grad_a = [(grad_mid[i] * mod[i][2]).astype(BF16) for i in both]
    full_ga = [spread(v) for v in grad_a]
    grad_att = [dot(v, proj_full).astype(BF16) for v in full_ga]
    g_proj_w = scatter_rows(weight_grad(full_ga, [out for out, _ in attended]))
    grad_qkv = [attend_back(qkv[i], grad_att[i], attended[i][1]) for i in both]
    grad_sa = [collect(dot(v, qkv_full, NT).astype(BF16)) for v in grad_qkv]
    g_qkv_w = scatter_rows(weight_grad(full_a, grad_qkv)).reshape(mod_rows, 3, local_width)
    grad_latent = jnp.stack(
        [
            grad_mid[i] + norm_back(*norm_a[i], grad_sa[i] * (1.0 + mod[i][1]))
            for i in both
        ],
        1,
    )

    mod_parts = jnp.stack(
        [
            jnp.stack(
                [
                    jnp.sum(grad_sa[i], 0),
                    jnp.sum(grad_sa[i] * norm_a[i][0], 0),
                    jnp.sum(grad_mid[i] * branch_a[i], 0),
                    jnp.sum(grad_sm[i], 0),
                    jnp.sum(grad_sm[i] * norm_m[i][0], 0),
                    jnp.sum(grad_y[i] * branch_m[i], 0),
                ],
                0,
            )
            for i in both
        ],
        0,
    )
    mod_cols = model_width // n_tensor
    by_cols = mod_parts.reshape(images, 6, n_tensor, mod_cols).transpose(2, 0, 1, 3)
    own_cols = jnp.sum(
        lax.all_to_all(by_cols, "tensor", 0, 0, tiled=True).reshape(by_cols.shape), 0
    )
    all_cols = lax.all_to_all(
        jnp.broadcast_to(own_cols[None], (n_dp,) + own_cols.shape), "dp", 0, 0, tiled=True
    ).reshape(n_dp * images, 6, mod_cols)
    g_mod_w = jnp.einsum(
        "gd,gke->dke", cond_cols, all_cols.astype(BF16), preferred_element_type=F32
    )
    g_mod_all = lax.all_gather(all_cols, "tensor", axis=2, tiled=True)
    g_mod_b = jnp.sum(g_mod_all, 0)
    act_rows = jnp.einsum(
        "gke,dke->gd", g_mod_all.astype(BF16), mod_weight, preferred_element_type=F32
    )
    grad_act = (
        lax.all_to_all(act_rows.reshape(n_dp, images, mod_rows), "dp", 0, 0, tiled=True)
        .reshape(n_dp, images, mod_rows)
        .transpose(1, 0, 2)
        .reshape(images, n_dp * mod_rows)
    )
    silu_out, silu_pull = jax.vjp(jax.nn.silu, cond_float)
    grad_cond = silu_pull(grad_act)[0]

    shared = jnp.concatenate(
        [
            sum(jnp.sum(v.astype(F32), 0) for v in grad_a),
            sum(jnp.sum(v.astype(F32), 0) for v in grad_m),
        ]
    )
    for bit in (1, 2):
        shared = shared + swap(shared, bit)
    biases = jnp.concatenate(
        [
            sum(jnp.sum(v.astype(F32), 0) for v in grad_qkv),
            sum(f[4][0] for f in ff),
            shared,
        ]
    )
    bit = 1
    while bit < n_dp:
        biases = biases + lax.ppermute(biases, "dp", [(i, i ^ bit) for i in range(n_dp)])
        bit *= 2
    cuts = [0, 3 * local_width]
    cuts.append(cuts[-1] + hidden_width)
    cuts.append(cuts[-1] + model_width)
    cuts.append(cuts[-1] + model_width)
    g_qkv_b, g_expand_b, g_proj_b, g_reduce_b = (
        biases[lo:hi] for lo, hi in zip(cuts, cuts[1:])
    )
    return (
        result,
        grad_latent,
        grad_cond,
        g_mod_w,
        g_mod_b,
        g_qkv_w,
        g_qkv_b.reshape(3, local_width),
        g_proj_w,
        g_proj_b,
        g_expand_w,
        g_expand_b,
        g_reduce_w,
        g_reduce_b,
    )


def solution(mesh):
    in_specs = (
        P("tensor", "dp", None),
        P("dp", None),
        P("dp", None, None),
        P(),
        P("dp", None, "tensor"),
        P(None, "tensor"),
        P("dp", "tensor"),
        P(),
        P("dp", "tensor"),
        P("tensor"),
        P("dp", "tensor"),
        P(),
        P("tensor", "dp", None),
    )
    out_specs = (
        P("tensor", "dp", None),
        P("tensor", "dp", None),
        P("dp", None),
        P("dp", None, "tensor"),
        P(),
        P("dp", None, "tensor"),
        P(None, "tensor"),
        P("dp", "tensor"),
        P(),
        P("dp", "tensor"),
        P("tensor"),
        P("dp", "tensor"),
        P(),
    )
    return jax.shard_map(
        per_device, mesh=mesh, in_specs=in_specs, out_specs=out_specs, check_vma=False
    )
```

```python
import functools

import jax
import jax.numpy as jnp
from jax import lax
from jax.experimental import pallas as pl
from jax.experimental.pallas import tpu as pltpu
from jax.sharding import PartitionSpec as P

HEAD_DIM = 64
F32 = jnp.float32
BF16 = jnp.bfloat16
LOG2E = 1.4426950408889634
GELU_C = 0.7978845608028654
GELU_A = 0.044715
NN = (((1,), (0,)), ((), ()))
NT = (((1,), (1,)), ((), ()))
TN = (((0,), (0,)), ((), ()))
SMALL_COST = pl.CostEstimate(flops=1000, bytes_accessed=1000, transcendentals=0)
VMEM_BYTES = 56 * 1024 * 1024


def dot(left, right, dims=NN):
    return lax.dot_general(left, right, dims, preferred_element_type=F32)


def params(*kinds):
    return pltpu.CompilerParams(dimension_semantics=kinds, vmem_limit_bytes=VMEM_BYTES)


def attend_kernel(chunk, q_ref, k_ref, v_ref, out_ref, lse_ref):
    length, width = q_ref.shape
    factor = HEAD_DIM ** (-0.5) * LOG2E
    values_t = v_ref[...].astype(F32).T.astype(BF16)
    keys = [k_ref[:, lo : lo + HEAD_DIM] for lo in range(0, width, HEAD_DIM)]

    def body(step, carry):
        rows = pl.ds(pl.multiple_of(step * chunk, chunk), chunk)
        outs = []
        for head, key in enumerate(keys):
            lo = head * HEAD_DIM
            scores = dot(key, q_ref[rows, lo : lo + HEAD_DIM], NT)
            top = jnp.max(scores, 0, keepdims=True)
            weights = jnp.exp2((scores - top) * factor)
            total = jnp.sum(weights, 0, keepdims=True)
            out_t = dot(values_t[lo : lo + HEAD_DIM], weights.astype(BF16))
            outs.append(out_t / total)
            lse_ref[0, head : head + 1, rows] = top * factor + jnp.log(total) * LOG2E
        out_ref[rows, :] = jnp.concatenate(outs, 0).T.astype(BF16)
        return carry

    lax.fori_loop(0, length // chunk, body, 0)


def attend(qkv):
    length, three = qkv.shape
    width = three // 3
    pairs = width // 128
    chunk = min(256, length)
    spec = lambda part: pl.BlockSpec((length, 128), lambda i: (0, part * pairs + i))
    return pl.pallas_call(
        functools.partial(attend_kernel, chunk),
        grid=(pairs,),
        in_specs=[spec(0), spec(1), spec(2)],
        out_specs=[
            pl.BlockSpec((length, 128), lambda i: (0, i)),
            pl.BlockSpec((1, 8, length), lambda i: (i, 0, 0)),
        ],
        out_shape=[
            jax.ShapeDtypeStruct((length, width), BF16),
            jax.ShapeDtypeStruct((pairs, 8, length), F32),
        ],
        compiler_params=params("arbitrary"),
        cost_estimate=SMALL_COST,
        name="attend",
    )(qkv, qkv, qkv)


def attend_back_kernel(chunk, q_ref, k_ref, v_ref, g_ref, lse_ref, out_ref, dk_ref, dv_ref):
    length, width = q_ref.shape
    total_width = out_ref.shape[1] // 3
    scale = HEAD_DIM ** (-0.5)
    factor = scale * LOG2E
    pair = pl.program_id(0)
    keys_t = k_ref[...].astype(F32).T.astype(BF16)
    heads = range(0, width, HEAD_DIM)
    keys = [k_ref[:, lo : lo + HEAD_DIM] for lo in heads]
    values = [v_ref[:, lo : lo + HEAD_DIM] for lo in heads]
    dk_ref[...] = jnp.zeros_like(dk_ref)
    dv_ref[...] = jnp.zeros_like(dv_ref)

    def columns(part):
        return pl.ds(pl.multiple_of(part * total_width + pair * width, width), width)

    def body(step, carry):
        rows = pl.ds(pl.multiple_of(step * chunk, chunk), chunk)
        outs = []
        for head, (key, value) in enumerate(zip(keys, values)):
            lo = head * HEAD_DIM
            query = q_ref[rows, lo : lo + HEAD_DIM]
            grad = g_ref[rows, lo : lo + HEAD_DIM]
            probs = jnp.exp2(dot(key, query, NT) * factor - lse_ref[0, head : head + 1, rows])
            dv_ref[head] += dot(probs.astype(BF16), grad)
            weighted = probs * dot(value, grad, NT)
            row_dot = jnp.sum(weighted, 0, keepdims=True)
            g_scores = (weighted - probs * row_dot).astype(BF16)
            dk_ref[head] += dot(g_scores, query)
            outs.append(dot(keys_t[lo : lo + HEAD_DIM], g_scores) * scale)
        out_ref[rows, columns(0)] = jnp.concatenate(outs, 0).T.astype(BF16)
        return carry

    lax.fori_loop(0, length // chunk, body, 0)
    n_heads = len(keys)
    out_ref[:, columns(1)] = (
        jnp.concatenate([dk_ref[h] for h in range(n_heads)], 1) * scale
    ).astype(BF16)
    out_ref[:, columns(2)] = jnp.concatenate([dv_ref[h] for h in range(n_heads)], 1).astype(BF16)


def attend_back(qkv, grad_att, lse):
    length, three = qkv.shape
    width = three // 3
    pairs = width // 128
    chunk = min(256, length)
    spec = lambda part: pl.BlockSpec((length, 128), lambda i: (0, part * pairs + i))
    return pl.pallas_call(
        functools.partial(attend_back_kernel, chunk),
        grid=(pairs,),
        in_specs=[
            spec(0),
            spec(1),
            spec(2),
            pl.BlockSpec((length, 128), lambda i: (0, i)),
            pl.BlockSpec((1, 8, length), lambda i: (i, 0, 0)),
        ],
        out_specs=pl.BlockSpec((length, three), lambda i: (0, 0)),
        out_shape=jax.ShapeDtypeStruct((length, three), BF16),
        scratch_shapes=[
            pltpu.VMEM((128 // HEAD_DIM, length, HEAD_DIM), F32),
            pltpu.VMEM((128 // HEAD_DIM, length, HEAD_DIM), F32),
        ],
        compiler_params=params("arbitrary"),
        cost_estimate=SMALL_COST,
        name="attend_back",
    )(qkv, qkv, qkv, grad_att, lse)


def norm_parts(values):
    centered = values - jnp.mean(values, -1, keepdims=True)
    scale = lax.rsqrt(jnp.mean(centered * centered, -1, keepdims=True) + 1e-06)
    return centered * scale, scale


def norm_back(normed, scale, grad):
    mean_g = jnp.mean(grad, -1, keepdims=True)
    mean_gn = jnp.mean(grad * normed, -1, keepdims=True)
    return scale * (grad - mean_g - normed * mean_gn)


def row(ref, index):
    return ref[index : index + 1, :]


def add_sums(ref, values):
    @pl.when(pl.program_id(0) == 0)
    def _():
        ref[...] = jnp.zeros_like(ref)

    for index, value in enumerate(values):
        ref[index : index + 1, :] += jnp.sum(value, 0, keepdims=True)


def total_of(near_ref, core_ref, chip_ref):
    near = near_ref[...].astype(F32) + core_ref[...].astype(F32)
    return near + chip_ref[...].astype(F32)


def middle_kernel(near, core, chip, x_ref, mod_ref, bias_ref, branch_ref, mid_ref, out_ref):
    branch = total_of(near, core, chip) + bias_ref[...].astype(F32)
    mid = x_ref[...].astype(F32) + row(mod_ref, 2) * branch
    normed, _ = norm_parts(mid)
    branch_ref[...] = branch
    mid_ref[...] = mid
    out_ref[...] = (normed * (1.0 + row(mod_ref, 4)) + row(mod_ref, 3)).astype(BF16)


def middle_back_kernel(
    near, core, chip, mid_ref, g_ref, branch_ref, mod_ref, gmid_ref, ga_ref, sums_ref
):
    g_sm = total_of(near, core, chip)
    normed, scale = norm_parts(mid_ref[...])
    g_mid = g_ref[...].astype(F32) + norm_back(normed, scale, g_sm * (1.0 + row(mod_ref, 4)))
    g_a = (g_mid * row(mod_ref, 2)).astype(BF16)
    gmid_ref[...] = g_mid
    ga_ref[...] = g_a
    add_sums(sums_ref, [g_sm, g_sm * normed, g_mid * branch_ref[...], g_a.astype(F32)])


def last_kernel(near, core, chip, x_ref, gmid_ref, mod_ref, out_ref, sums_ref):
    g_sa = total_of(near, core, chip)
    normed, scale = norm_parts(x_ref[...].astype(F32))
    out_ref[...] = gmid_ref[...] + norm_back(normed, scale, g_sa * (1.0 + row(mod_ref, 1)))
    add_sums(sums_ref, [g_sa, g_sa * normed])


def result_kernel(near, core, chip, mid_ref, g_ref, mod_ref, bias_ref, out_ref, sums_ref):
    branch = total_of(near, core, chip) + bias_ref[...].astype(F32)
    grad = g_ref[...].astype(F32)
    out_ref[...] = (mid_ref[...] + row(mod_ref, 5) * branch).astype(BF16)
    g_m = (grad * row(mod_ref, 5)).astype(BF16).astype(F32)
    add_sums(sums_ref, [grad * branch, g_m])


def by_rows(kernel, name, tall, wide, outs, sums):
    count, width = tall[-1].shape
    tile = min(128, count)
    tiled = pl.BlockSpec((tile, width), lambda i: (i, 0))
    out_specs = [tiled] * len(outs)
    out_shape = [jax.ShapeDtypeStruct((count, width), t) for t in outs]
    if sums:
        out_specs.append(pl.BlockSpec((8, width), lambda i: (0, 0)))
        out_shape.append(jax.ShapeDtypeStruct((8, width), F32))
    return pl.pallas_call(
        kernel,
        grid=(count // tile,),
        in_specs=[tiled] * len(tall) + [pl.BlockSpec(w.shape, lambda i: (0, 0)) for w in wide],
        out_specs=out_specs,
        out_shape=out_shape,
        compiler_params=params("arbitrary"),
        cost_estimate=SMALL_COST,
        name=name,
    )(*tall, *wide)


def two_parts(tile, width):
    return [
        pl.BlockSpec((tile, width), lambda i: (jnp.minimum(i, 1), 0)),
        pl.BlockSpec((tile, width), lambda i: (jnp.maximum(i - 2, 0), 0)),
    ]


def pick(first_ref, second_ref):
    return jnp.where(pl.program_id(0) < 2, first_ref[...], second_ref[...])


def put(first_ref, second_ref, value):
    @pl.when(pl.program_id(0) < 2)
    def _():
        first_ref[...] = value

    @pl.when(pl.program_id(0) >= 2)
    def _():
        second_ref[...] = value


def norm_project_kernel(xa_ref, xb_ref, mod_ref, w_ref, bias_ref, shifted_ref, out_ref):
    normed, _ = norm_parts(pick(xa_ref, xb_ref).astype(F32))
    shifted = (normed * (1.0 + row(mod_ref, 1)) + row(mod_ref, 0)).astype(BF16)
    shifted_ref[...] = shifted
    out_ref[...] = (dot(shifted, w_ref[...]) + bias_ref[...].astype(F32)).astype(BF16)


def norm_project(pieces, mod, weight, bias):
    count, width = pieces[0].shape
    tokens, tile = 2 * count, count // 2
    outs = bias.shape[1]
    whole = lambda r, c: pl.BlockSpec((r, c), lambda i: (0, 0))
    return pl.pallas_call(
        norm_project_kernel,
        grid=(4,),
        in_specs=two_parts(tile, width) + [whole(*mod.shape), whole(width, outs), whole(1, outs)],
        out_specs=[pl.BlockSpec((tile, c), lambda i: (i, 0)) for c in (width, outs)],
        out_shape=[jax.ShapeDtypeStruct((tokens, c), BF16) for c in (width, outs)],
        compiler_params=params("arbitrary"),
        cost_estimate=SMALL_COST,
        name="norm_project",
    )(*pieces, mod, weight, bias)


def row_sums_kernel(pa_ref, pb_ref, xa_ref, xb_ref, sums_ref):
    part = pick(pa_ref, pb_ref).astype(F32)
    normed, _ = norm_parts(pick(xa_ref, xb_ref).astype(F32))
    add_sums(sums_ref, [part, part * normed])


def row_sums(parts, rows):
    count, width = parts[0].shape
    tile = count // 2
    return pl.pallas_call(
        row_sums_kernel,
        grid=(4,),
        in_specs=two_parts(tile, width) + two_parts(tile, width),
        out_specs=pl.BlockSpec((8, width), lambda i: (0, 0)),
        out_shape=jax.ShapeDtypeStruct((8, width), F32),
        compiler_params=params("arbitrary"),
        cost_estimate=SMALL_COST,
        name="row_sums",
    )(*parts, *rows)


def project(x, weight):
    half = x.shape[0] // 2
    far = dot(x[half:], weight, NT).astype(BF16)
    return dot(x[:half], weight, NT).astype(BF16), far


def weight_grad_kernel(n_jobs, *refs):
    out_ref = refs[-1]
    for job in range(n_jobs):
        left_a, left_b, right_a, right_b = refs[4 * job : 4 * job + 4]

        @pl.when(pl.program_id(0) == job)
        def _():
            total = dot(left_a[...], right_a[...], TN) + dot(left_b[...], right_b[...], TN)
            out_ref[...] = total.astype(BF16)


def weight_grad(*jobs):
    tokens, rows = jobs[0][0][0].shape
    width = jobs[0][1][0].shape[1]
    tile = min(256, rows)
    steps = rows // tile

    def left_spec(job):
        def index(j, i):
            return 0, jnp.where(j == job, i, jnp.where(j < job, 0, steps - 1))

        return pl.BlockSpec((tokens, tile), index)

    in_specs, operands = [], []
    for job, (lefts, rights) in enumerate(jobs):
        in_specs += [left_spec(job)] * 2
        in_specs += [pl.BlockSpec((tokens, width), lambda j, i: (0, 0))] * 2
        operands += list(lefts) + list(rights)
    return pl.pallas_call(
        functools.partial(weight_grad_kernel, len(jobs)),
        grid=(len(jobs), steps),
        in_specs=in_specs,
        out_specs=pl.BlockSpec((tile, width), lambda j, i: (i, j)),
        out_shape=jax.ShapeDtypeStruct((rows, len(jobs) * width), BF16),
        compiler_params=params("arbitrary", "arbitrary"),
        cost_estimate=SMALL_COST,
        name="weight_grad",
    )(*operands)


def mlp_kernel(
    xa_ref, xb_ref, ga_ref, gb_ref, mod_ref, up_ref, down_ref, bias_ref,
    x_out, g_out, hid_ref, gpre_ref, near_ref, far_ref, gnear_ref, gfar_ref, gbias_ref,
):
    x = pick(xa_ref, xb_ref)
    grad = (pick(ga_ref, gb_ref).astype(F32) * row(mod_ref, 5)).astype(BF16)
    x_out[...] = x
    g_out[...] = grad
    pre = dot(x, up_ref[...]) + bias_ref[...].astype(F32)
    square = pre * pre
    th = jnp.tanh(GELU_C * pre * (1.0 + GELU_A * square))
    half = 0.5 * (1.0 + th)
    hidden = (pre * half).astype(BF16)
    slope = half + (0.5 * GELU_C) * pre * (1.0 - th * th) * (1.0 + 3.0 * GELU_A * square)
    g_pre = (dot(grad, down_ref[...]) * slope).astype(BF16)
    hid_ref[...] = hidden
    gpre_ref[...] = g_pre
    put(gnear_ref, gfar_ref, dot(g_pre, up_ref[...], NT).astype(BF16))
    put(near_ref, far_ref, dot(hidden, down_ref[...], NT).astype(BF16))
    add_sums(gbias_ref, [g_pre.astype(F32)])


def mlp(x_pieces, g_pieces, mod, weights, bias):
    count, width = x_pieces[0].shape
    tokens, tile = 2 * count, count // 2
    hidden = bias.shape[1]
    rows = lambda cols: pl.BlockSpec((tile, cols), lambda i: (i, 0))
    whole = lambda r, c: pl.BlockSpec((r, c), lambda i: (0, 0))
    return pl.pallas_call(
        mlp_kernel,
        grid=(4,),
        in_specs=two_parts(tile, width)
        + two_parts(tile, width)
        + [
            whole(*mod.shape),
            pl.BlockSpec((width, hidden), lambda i: (0, 0)),
            pl.BlockSpec((width, hidden), lambda i: (0, 1)),
            whole(1, hidden),
        ],
        out_specs=[rows(width), rows(width), rows(hidden), rows(hidden)]
        + two_parts(tile, width)
        + two_parts(tile, width)
        + [whole(8, hidden)],
        out_shape=[
            jax.ShapeDtypeStruct((tokens, width), BF16),
            jax.ShapeDtypeStruct((tokens, width), BF16),
            jax.ShapeDtypeStruct((tokens, hidden), BF16),
            jax.ShapeDtypeStruct((tokens, hidden), BF16),
        ]
        + [jax.ShapeDtypeStruct((count, width), BF16)] * 4
        + [jax.ShapeDtypeStruct((8, hidden), F32)],
        compiler_params=params("arbitrary"),
        cost_estimate=SMALL_COST,
        name="feed_forward",
    )(*x_pieces, *g_pieces, mod, weights, weights, bias)


def swap(value, bit):
    n = lax.axis_size("tensor")
    return lax.ppermute(value, "tensor", [(i, i ^ bit) for i in range(n)])


def joined(*values):
    return lax.optimization_barrier(values)


def after(value, token):
    return lax.optimization_barrier((value, token))[0]


def with_core(near, core):
    count = near.shape[0] // 2
    return (near[count:].astype(F32) + core[count:].astype(F32)).astype(BF16)


def exchange(value):
    return lax.all_to_all(value, "dp", 0, 0, tiled=True).reshape(value.shape)


def per_device(
    latents,
    conditioning,
    mod_weight,
    mod_bias,
    qkv_weight,
    qkv_bias,
    proj_weight,
    proj_bias,
    expand_weight,
    expand_bias,
    reduce_weight,
    reduce_bias,
    out_grad,
):
    n_tensor = lax.axis_size("tensor")
    n_dp = lax.axis_size("dp")
    row_count, images, model_width = latents.shape
    local_width = qkv_weight.shape[2]
    hidden_width = expand_weight.shape[1]
    mod_rows = mod_weight.shape[0]
    both = range(images)

    attn_full = lax.all_gather(
        jnp.concatenate([qkv_weight.reshape(mod_rows, 3 * local_width), proj_weight], 1),
        "dp",
        axis=0,
        tiled=True,
    )
    qkv_full, proj_full = attn_full[:, : 3 * local_width], attn_full[:, 3 * local_width :]
    x = [latents[:, i] for i in both]
    grad_y = [out_grad[:, i] for i in both]
    recv_x0 = swap(x[0], 2)

    cond_float = conditioning.astype(F32)
    cond_low = jax.nn.silu(cond_float).astype(BF16)
    cond_cols = exchange(
        cond_low.reshape(images, n_dp, mod_rows).transpose(1, 0, 2)
    ).reshape(n_dp * images, mod_rows)
    mod_part = jnp.einsum("gd,dke->gke", cond_cols, mod_weight, preferred_element_type=F32)
    mod_part, recv_x0 = joined(mod_part, recv_x0)
    recv_x1 = swap(after(x[1], recv_x0), 2)
    mod_recv = exchange(mod_part.reshape(n_dp, images, 6, model_width))
    pair_x0 = jnp.concatenate([x[0], recv_x0])
    core_x0 = swap(pair_x0, 1)
    mod_recv, core_x0, recv_x1 = joined(mod_recv, core_x0, recv_x1)
    recv_g = swap(after(out_grad, recv_x1), 2)
    pair_x = [pair_x0, jnp.concatenate([x[1], recv_x1])]
    core_x1 = swap(pair_x[1], 1)
    modulation = jnp.sum(mod_recv, 0) + mod_bias.astype(F32)[None]
    mod = [modulation[i] for i in both]

    ff_full = lax.all_gather(
        after(jnp.concatenate([expand_weight, reduce_weight], 1), modulation),
        "dp",
        axis=0,
        tiled=True,
    )

    bias_qkv = qkv_bias.reshape(1, 3 * local_width)
    bias_row = proj_bias.reshape(1, model_width)
    bias_out = reduce_bias.reshape(1, model_width)
    bias_hidden = expand_bias.reshape(1, hidden_width)

    def middle(i, pieces):
        return by_rows(
            middle_kernel,
            "middle",
            list(pieces) + [x[i]],
            [mod[i], bias_row],
            [F32, F32, BF16],
            False,
        )

    sh0, qkv0 = norm_project((pair_x[0], core_x0), mod[0], attn_full, bias_qkv)
    att0, lse0 = attend(qkv0)
    att0, recv_g, core_x1 = joined(att0, recv_g, core_x1)
    near0, far0 = project(att0, proj_full)
    core0 = swap(far0, 1)
    sh1, qkv1 = norm_project((after(pair_x[1], near0), core_x1), mod[1], attn_full, bias_qkv)
    qkv1, core0 = joined(qkv1, core0)
    chip0 = with_core(near0, core0)
    recv0 = swap(chip0, 2)
    pair_g = [jnp.concatenate([grad_y[i], recv_g[:, i]]) for i in both]
    core_g = [swap(v, 1) for v in pair_g]
    att1, lse1 = attend(after(qkv1, (chip0, pair_g)))
    att1, recv0, core_g = joined(att1, recv0, core_g)
    branch0, mid0, low0 = middle(0, (near0, core0, recv0))
    recv_m0 = swap(low0, 2)
    near1, far1 = project(after(att1, low0), proj_full)
    core1 = swap(far1, 1)
    recv1 = swap(with_core(near1, core1), 2)
    recv1, recv_m0 = joined(recv1, recv_m0)
    pair_m0 = jnp.concatenate([low0, recv_m0])
    core_m0 = swap(pair_m0, 1)
    branch1, mid1, low1 = middle(1, (near1, core1, recv1))
    low1, core_m0 = joined(low1, core_m0)
    recv_m1 = swap(low1, 2)
    shifted_a, attended, lse = [sh0, sh1], [att0, att1], [lse0, lse1]
    branch_a, mid = [branch0, branch1], [mid0, mid1]

    def feed(i, pieces):
        return mlp(pieces, (pair_g[i], core_g[i]), mod[i], ff_full, bias_hidden)

    ff0 = feed(0, (after(pair_m0, low1), core_m0))
    ff0, recv_m1 = joined(ff0, recv_m1)
    core0 = swap(ff0[7], 1)
    pair_m1 = jnp.concatenate([low1, recv_m1])
    core_m1 = swap(pair_m1, 1)
    chip0 = with_core(ff0[6], core0)
    recv0 = swap(chip0, 2)
    ff1 = feed(1, after((pair_m1, core_m1), chip0))
    ff1, recv0 = joined(ff1, recv0)
    ff = [ff0, ff1]

    def middle_back(i, pieces):
        return by_rows(
            middle_back_kernel,
            "middle_back",
            list(pieces) + [mid[i], grad_y[i], branch_a[i]],
            [mod[i]],
            [F32, BF16],
            True,
        )

    core1 = swap(ff1[7], 1)
    gmid0, ga0, sums_m0 = middle_back(0, (ff0[6], core0, recv0))
    ga0, core1 = joined(ga0, core1)
    recv_ga0 = swap(ga0, 2)
    chip1 = with_core(ff1[6], core1)
    recv1 = swap(chip1, 2)
    core_b = [swap(after(f[5], ga0), 1) for f in ff]
    x_parts, g_parts = after(([f[0] for f in ff], [f[1] for f in ff]), (ga0, chip1))
    g_ff = weight_grad((x_parts, [f[3] for f in ff]), (g_parts, [f[2] for f in ff]))
    g_ff, recv_ga0, recv1, core_b = joined(g_ff, recv_ga0, recv1, core_b)
    g_ff_w = lax.psum_scatter(g_ff, "dp", scatter_dimension=0, tiled=True).astype(F32)
    g_expand_w, g_reduce_w = g_ff_w[:, :hidden_width], g_ff_w[:, hidden_width:]
    pair_ga0 = jnp.concatenate([ga0, recv_ga0])
    core_ga0 = swap(pair_ga0, 1)
    gmid1, ga1, sums_m1 = middle_back(1, (ff1[6], core1, recv1))
    ga1, core_ga0 = joined(ga1, core_ga0)
    recv_ga1 = swap(ga1, 2)
    full_ga0 = jnp.concatenate([after(pair_ga0, ga1), core_ga0])
    grad_mid, grad_a, sums_m = [gmid0, gmid1], [ga0, ga1], [sums_m0, sums_m1]

    def finish(i, pieces):
        return by_rows(
            result_kernel,
            "result",
            list(pieces) + [mid[i], grad_y[i]],
            [mod[i], bias_out],
            [BF16],
            True,
        )

    chip_b = [with_core(ff[i][4], core_b[i]) for i in both]
    recv_b0 = swap(after(chip_b[0], ga1), 2)
    gatt0 = dot(full_ga0, proj_full).astype(BF16)
    gqkv0 = attend_back(qkv0, after(gatt0, chip_b), lse0)
    gqkv0, recv_ga1, recv_b0 = joined(gqkv0, recv_ga1, recv_b0)
    pair_ga1 = jnp.concatenate([ga1, recv_ga1])
    core_ga1 = swap(pair_ga1, 1)
    near0, far0 = project(gqkv0, qkv_full)
    near0, far0, core_ga1 = joined(near0, far0, core_ga1)
    core0 = swap(far0, 1)
    full_ga = [full_ga0, jnp.concatenate([pair_ga1, core_ga1])]
    g_proj = weight_grad((after(full_ga, far0), attended))
    res0, sums_r0 = finish(0, (ff0[4], core_b[0], after(recv_b0, far0)))
    g_proj, res0, core0 = joined(g_proj, res0, core0)
    chip0 = with_core(near0, core0)
    recv0 = swap(chip0, 2)
    recv_b1 = swap(after(chip_b[1], chip0), 2)
    gatt1 = dot(after(full_ga[1], chip0), proj_full).astype(BF16)
    pieces_p = exchange(g_proj.reshape(n_dp, -1, local_width))
    gqkv1 = attend_back(qkv1, after(gatt1, chip0), lse1)
    gqkv1, recv0, recv_b1, pieces_p = joined(gqkv1, recv0, recv_b1, pieces_p)
    g_proj_w = jnp.sum(pieces_p.astype(F32), 0)
    grad_qkv = [gqkv0, gqkv1]
    g_qkv = weight_grad((shifted_a, grad_qkv))
    g_qkv_w = lax.psum_scatter(g_qkv, "dp", scatter_dimension=0, tiled=True)
    near1, far1 = project(after(gqkv1, g_qkv), qkv_full)
    core1 = swap(far1, 1)
    sums_p1 = row_sums(after((near1, far1), g_ff_w), (pair_x[1], core_x1))
    sums_p1, core1 = joined(sums_p1, core1)

    def last(i, pieces):
        return by_rows(
            last_kernel, "last", list(pieces) + [x[i], grad_mid[i]], [mod[i]], [F32], True
        )

    lat0, sums_a0 = last(0, (near0, core0, after(recv0, sums_p1)))
    res1, sums_r1 = finish(1, (ff1[4], core_b[1], after(recv_b1, sums_p1)))
    sums_a, sums_r = [sums_a0, sums_p1], [sums_r0, sums_r1]

    shared = jnp.concatenate(
        [jnp.concatenate([sums_a[i][:2], sums_m[i][2:3], sums_m[i][:2], sums_r[i][:1]]) for i in both]
        + [sum(s[3:4] for s in sums_m), sum(s[1:2] for s in sums_r)]
    )
    shared = shared + swap(shared, 1)
    chip1 = with_core(near1, core1)
    recv1 = swap(after(chip1, shared), 2)
    shared = shared + swap(shared, 2)
    local = jnp.concatenate(
        [
            sum(jnp.sum(v.astype(F32), 0) for v in grad_qkv),
            sum(f[8][0] for f in ff),
        ]
    )
    n_mod = images * 6 * model_width
    shared = shared.reshape(-1)
    local = jnp.concatenate([shared[n_mod:], local])
    high = local.astype(BF16)
    mine = jnp.concatenate(
        [shared[:n_mod].astype(BF16), high, (local - high.astype(F32)).astype(BF16)]
    )
    everyone = exchange(jnp.broadcast_to(mine[None], (n_dp,) + mine.shape)).astype(F32)
    lat1 = last(1, (near1, core1, recv1))[0]
    grad_latent, result = [lat0, lat1], [res0, res1]
    g_mod_all = everyone[:, :n_mod].reshape(n_dp * images, 6, model_width)
    biases = jnp.sum(everyone[:, n_mod:].reshape(n_dp, 2, -1), (0, 1))
    sizes = [model_width, model_width, 3 * local_width, hidden_width]
    cuts = [sum(sizes[:n]) for n in range(len(sizes) + 1)]
    g_proj_b, g_reduce_b, g_qkv_b, g_expand_b = (
        biases[lo:hi] for lo, hi in zip(cuts, cuts[1:])
    )

    g_mod_b = jnp.sum(g_mod_all, 0)
    g_mod_low = g_mod_all.astype(BF16)
    mod_cols = model_width // n_tensor
    own_cols = lax.dynamic_slice_in_dim(
        g_mod_low, lax.axis_index("tensor") * mod_cols, mod_cols, 2
    )
    g_mod_w = jnp.einsum("gd,gke->dke", cond_cols, own_cols, preferred_element_type=F32)
    act_rows = jnp.einsum("gke,dke->gd", g_mod_low, mod_weight, preferred_element_type=F32)
    grad_act = (
        exchange(act_rows.reshape(n_dp, images, mod_rows))
        .transpose(1, 0, 2)
        .reshape(images, n_dp * mod_rows)
    )
    silu_out, silu_pull = jax.vjp(jax.nn.silu, cond_float)
    grad_cond = silu_pull(grad_act)[0]
    g_qkv_w = after(g_qkv_w, (grad_cond, grad_latent, g_mod_w)).astype(F32)
    g_qkv_w = g_qkv_w.reshape(mod_rows, 3, local_width)
    return (
        jnp.stack(result, 1),
        jnp.stack(grad_latent, 1),
        grad_cond,
        g_mod_w,
        g_mod_b,
        g_qkv_w,
        g_qkv_b.reshape(3, local_width),
        g_proj_w,
        g_proj_b,
        g_expand_w,
        g_expand_b,
        g_reduce_w,
        g_reduce_b,
    )


def solution(mesh):
    in_specs = (
        P("tensor", "dp", None),
        P("dp", None),
        P("dp", None, None),
        P(),
        P("dp", None, "tensor"),
        P(None, "tensor"),
        P("dp", "tensor"),
        P(),
        P("dp", "tensor"),
        P("tensor"),
        P("dp", "tensor"),
        P(),
        P("tensor", "dp", None),
    )
    out_specs = (
        P("tensor", "dp", None),
        P("tensor", "dp", None),
        P("dp", None),
        P("dp", None, "tensor"),
        P(),
        P("dp", None, "tensor"),
        P(None, "tensor"),
        P("dp", "tensor"),
        P(),
        P("dp", "tensor"),
        P("tensor"),
        P("dp", "tensor"),
        P(),
    )
    return jax.shard_map(
        per_device, mesh=mesh, in_specs=in_specs, out_specs=out_specs, check_vma=False
    )
```

```python
import functools

import jax
import jax.numpy as jnp
from jax import lax
from jax.experimental import pallas as pl
from jax.experimental.pallas import tpu as pltpu
from jax.sharding import PartitionSpec as P

HEAD_DIM = 64
F32 = jnp.float32
BF16 = jnp.bfloat16
LOG2E = 1.4426950408889634
GELU_C = 0.7978845608028654
GELU_A = 0.044715
NN = (((1,), (0,)), ((), ()))
NT = (((1,), (1,)), ((), ()))
TN = (((0,), (0,)), ((), ()))
SMALL_COST = pl.CostEstimate(flops=1000, bytes_accessed=1000, transcendentals=0)
HALF_STEPS = 2
VMEM_BYTES = 56 * 1024 * 1024


def dot(left, right, dims=NN):
    return lax.dot_general(left, right, dims, preferred_element_type=F32)


def params(*kinds):
    return pltpu.CompilerParams(dimension_semantics=kinds, vmem_limit_bytes=VMEM_BYTES)


def attend_kernel(chunk, q_ref, k_ref, v_ref, out_ref, lse_ref):
    length, width = q_ref.shape
    factor = HEAD_DIM ** (-0.5) * LOG2E
    values_t = v_ref[...].astype(F32).T.astype(BF16)
    keys = [k_ref[:, lo : lo + HEAD_DIM] for lo in range(0, width, HEAD_DIM)]

    def body(step, carry):
        rows = pl.ds(pl.multiple_of(step * chunk, chunk), chunk)
        outs = []
        for head, key in enumerate(keys):
            lo = head * HEAD_DIM
            scores = dot(key, q_ref[rows, lo : lo + HEAD_DIM], NT)
            top = jnp.max(scores, 0, keepdims=True)
            weights = jnp.exp2((scores - top) * factor)
            total = jnp.sum(weights, 0, keepdims=True)
            out_t = dot(values_t[lo : lo + HEAD_DIM], weights.astype(BF16))
            outs.append(out_t / total)
            lse_ref[0, head : head + 1, rows] = top * factor + jnp.log(total) * LOG2E
        out_ref[rows, :] = jnp.concatenate(outs, 0).T.astype(BF16)
        return carry

    lax.fori_loop(0, length // chunk, body, 0, unroll=True)


def attend(qkv):
    length, three = qkv.shape
    width = three // 3
    pairs = width // 128
    chunk = min(1024, length)
    spec = lambda part: pl.BlockSpec((length, 128), lambda i: (0, part * pairs + i))
    return pl.pallas_call(
        functools.partial(attend_kernel, chunk),
        grid=(pairs,),
        in_specs=[spec(0), spec(1), spec(2)],
        out_specs=[
            pl.BlockSpec((length, 128), lambda i: (0, i)),
            pl.BlockSpec((1, 8, length), lambda i: (i, 0, 0)),
        ],
        out_shape=[
            jax.ShapeDtypeStruct((length, width), BF16),
            jax.ShapeDtypeStruct((pairs, 8, length), F32),
        ],
        compiler_params=params("arbitrary"),
        cost_estimate=SMALL_COST,
        name="attend",
    )(qkv, qkv, qkv)


def attend_back_kernel(chunk, q_ref, k_ref, v_ref, g_ref, lse_ref, out_ref, dk_ref, dv_ref):
    length, width = q_ref.shape
    total_width = out_ref.shape[1] // 3
    scale = HEAD_DIM ** (-0.5)
    factor = scale * LOG2E
    pair = pl.program_id(0)
    keys_t = k_ref[...].astype(F32).T.astype(BF16)
    heads = range(0, width, HEAD_DIM)
    keys = [k_ref[:, lo : lo + HEAD_DIM] for lo in heads]
    values = [v_ref[:, lo : lo + HEAD_DIM] for lo in heads]
    dk_ref[...] = jnp.zeros_like(dk_ref)
    dv_ref[...] = jnp.zeros_like(dv_ref)

    def columns(part):
        return pl.ds(pl.multiple_of(part * total_width + pair * width, width), width)

    def body(step, carry):
        rows = pl.ds(pl.multiple_of(step * chunk, chunk), chunk)
        outs = []
        for head, (key, value) in enumerate(zip(keys, values)):
            lo = head * HEAD_DIM
            query = q_ref[rows, lo : lo + HEAD_DIM]
            grad = g_ref[rows, lo : lo + HEAD_DIM]
            probs = jnp.exp2(dot(key, query, NT) * factor - lse_ref[0, head : head + 1, rows])
            dv_ref[head] += dot(probs.astype(BF16), grad)
            weighted = probs * dot(value, grad, NT)
            row_dot = jnp.sum(weighted, 0, keepdims=True)
            g_scores = (weighted - probs * row_dot).astype(BF16)
            dk_ref[head] += dot(g_scores, query)
            outs.append(dot(keys_t[lo : lo + HEAD_DIM], g_scores) * scale)
        out_ref[rows, columns(0)] = jnp.concatenate(outs, 0).T.astype(BF16)
        return carry

    lax.fori_loop(0, length // chunk, body, 0, unroll=True)
    n_heads = len(keys)
    out_ref[:, columns(1)] = (
        jnp.concatenate([dk_ref[h] for h in range(n_heads)], 1) * scale
    ).astype(BF16)
    out_ref[:, columns(2)] = jnp.concatenate([dv_ref[h] for h in range(n_heads)], 1).astype(BF16)


def attend_back(qkv, grad_att, lse):
    length, three = qkv.shape
    width = three // 3
    pairs = width // 128
    chunk = min(1024, length)
    spec = lambda part: pl.BlockSpec((length, 128), lambda i: (0, part * pairs + i))
    return pl.pallas_call(
        functools.partial(attend_back_kernel, chunk),
        grid=(pairs,),
        in_specs=[
            spec(0),
            spec(1),
            spec(2),
            pl.BlockSpec((length, 128), lambda i: (0, i)),
            pl.BlockSpec((1, 8, length), lambda i: (i, 0, 0)),
        ],
        out_specs=pl.BlockSpec((length, three), lambda i: (0, 0)),
        out_shape=jax.ShapeDtypeStruct((length, three), BF16),
        scratch_shapes=[
            pltpu.VMEM((128 // HEAD_DIM, length, HEAD_DIM), F32),
            pltpu.VMEM((128 // HEAD_DIM, length, HEAD_DIM), F32),
        ],
        compiler_params=params("arbitrary"),
        cost_estimate=SMALL_COST,
        name="attend_back",
    )(qkv, qkv, qkv, grad_att, lse)


def norm_parts(values):
    centered = values - jnp.mean(values, -1, keepdims=True)
    scale = lax.rsqrt(jnp.mean(centered * centered, -1, keepdims=True) + 1e-06)
    return centered * scale, scale


def norm_back(normed, scale, grad):
    mean_g = jnp.mean(grad, -1, keepdims=True)
    mean_gn = jnp.mean(grad * normed, -1, keepdims=True)
    return scale * (grad - mean_g - normed * mean_gn)


def row(ref, index):
    return ref[index : index + 1, :]


def add_sums(ref, values):
    @pl.when(pl.program_id(0) == 0)
    def _():
        ref[...] = jnp.zeros_like(ref)

    for index, value in enumerate(values):
        ref[index : index + 1, :] += jnp.sum(value, 0, keepdims=True)


def total_of(near_ref, core_ref, chip_ref):
    near = near_ref[...].astype(F32) + core_ref[...].astype(F32)
    return near + chip_ref[...].astype(F32)


def middle_kernel(near, core, chip, x_ref, mod_ref, bias_ref, branch_ref, mid_ref, out_ref):
    branch = total_of(near, core, chip) + bias_ref[...].astype(F32)
    mid = x_ref[...].astype(F32) + row(mod_ref, 2) * branch
    normed, _ = norm_parts(mid)
    branch_ref[...] = branch
    mid_ref[...] = mid
    out_ref[...] = (normed * (1.0 + row(mod_ref, 4)) + row(mod_ref, 3)).astype(BF16)


def middle_back_kernel(
    near, core, chip, mid_ref, g_ref, branch_ref, mod_ref, gmid_ref, ga_ref, sums_ref
):
    g_sm = total_of(near, core, chip)
    normed, scale = norm_parts(mid_ref[...])
    g_mid = g_ref[...].astype(F32) + norm_back(normed, scale, g_sm * (1.0 + row(mod_ref, 4)))
    g_a = (g_mid * row(mod_ref, 2)).astype(BF16)
    gmid_ref[...] = g_mid
    ga_ref[...] = g_a
    add_sums(sums_ref, [g_sm, g_sm * normed, g_mid * branch_ref[...], g_a.astype(F32)])


def last_kernel(near, core, chip, x_ref, gmid_ref, mod_ref, out_ref, sums_ref):
    g_sa = total_of(near, core, chip)
    normed, scale = norm_parts(x_ref[...].astype(F32))
    out_ref[...] = gmid_ref[...] + norm_back(normed, scale, g_sa * (1.0 + row(mod_ref, 1)))
    add_sums(sums_ref, [g_sa, g_sa * normed])


def result_kernel(near, core, chip, mid_ref, mod_ref, bias_ref, out_ref):
    branch = total_of(near, core, chip) + bias_ref[...].astype(F32)
    out_ref[...] = (mid_ref[...] + row(mod_ref, 5) * branch).astype(BF16)


def by_rows(kernel, name, tall, wide, outs, sums):
    count, width = tall[-1].shape
    tile = min(128, count)
    tiled = pl.BlockSpec((tile, width), lambda i: (i, 0))
    out_specs = [tiled] * len(outs)
    out_shape = [jax.ShapeDtypeStruct((count, width), t) for t in outs]
    if sums:
        out_specs.append(pl.BlockSpec((8, width), lambda i: (0, 0)))
        out_shape.append(jax.ShapeDtypeStruct((8, width), F32))
    return pl.pallas_call(
        kernel,
        grid=(count // tile,),
        in_specs=[tiled] * len(tall) + [pl.BlockSpec(w.shape, lambda i: (0, 0)) for w in wide],
        out_specs=out_specs,
        out_shape=out_shape,
        compiler_params=params("arbitrary"),
        cost_estimate=SMALL_COST,
        name=name,
    )(*tall, *wide)


def two_parts(tile, width):
    return [
        pl.BlockSpec((tile, width), lambda i: (jnp.minimum(i, HALF_STEPS - 1), 0)),
        pl.BlockSpec((tile, width), lambda i: (jnp.maximum(i - HALF_STEPS, 0), 0)),
    ]


def pick(first_ref, second_ref):
    return jnp.where(pl.program_id(0) < HALF_STEPS, first_ref[...], second_ref[...])


def put(first_ref, second_ref, value):
    @pl.when(pl.program_id(0) < HALF_STEPS)
    def _():
        first_ref[...] = value

    @pl.when(pl.program_id(0) >= HALF_STEPS)
    def _():
        second_ref[...] = value


def norm_project_kernel(xa_ref, xb_ref, mod_ref, w_ref, bias_ref, shifted_ref, out_ref):
    normed, _ = norm_parts(pick(xa_ref, xb_ref).astype(F32))
    shifted = (normed * (1.0 + row(mod_ref, 1)) + row(mod_ref, 0)).astype(BF16)
    shifted_ref[...] = shifted
    out_ref[...] = (dot(shifted, w_ref[...]) + bias_ref[...].astype(F32)).astype(BF16)


def norm_project(pieces, mod, weight, bias):
    count, width = pieces[0].shape
    tokens, tile = 2 * count, count // HALF_STEPS
    outs = bias.shape[1]
    whole = lambda r, c: pl.BlockSpec((r, c), lambda i: (0, 0))
    return pl.pallas_call(
        norm_project_kernel,
        grid=(2 * HALF_STEPS,),
        in_specs=two_parts(tile, width) + [whole(*mod.shape), whole(width, outs), whole(1, outs)],
        out_specs=[pl.BlockSpec((tile, c), lambda i: (i, 0)) for c in (width, outs)],
        out_shape=[jax.ShapeDtypeStruct((tokens, c), BF16) for c in (width, outs)],
        compiler_params=params("arbitrary"),
        cost_estimate=SMALL_COST,
        name="norm_project",
    )(*pieces, mod, weight, bias)


def row_sums_kernel(pa_ref, pb_ref, xa_ref, xb_ref, sums_ref):
    part = pick(pa_ref, pb_ref).astype(F32)
    normed, _ = norm_parts(pick(xa_ref, xb_ref).astype(F32))
    add_sums(sums_ref, [part, part * normed])


def row_sums(parts, rows):
    count, width = parts[0].shape
    tile = count // HALF_STEPS
    return pl.pallas_call(
        row_sums_kernel,
        grid=(2 * HALF_STEPS,),
        in_specs=two_parts(tile, width) + two_parts(tile, width),
        out_specs=pl.BlockSpec((8, width), lambda i: (0, 0)),
        out_shape=jax.ShapeDtypeStruct((8, width), F32),
        compiler_params=params("arbitrary"),
        cost_estimate=SMALL_COST,
        name="row_sums",
    )(*parts, *rows)


def project(x, weight):
    half = x.shape[0] // 2
    far = dot(x[half:], weight, NT).astype(BF16)
    return dot(x[:half], weight, NT).astype(BF16), far


def weight_grad_kernel(n_jobs, *refs):
    out_ref = refs[-1]
    for job in range(n_jobs):
        left_a, left_b, right_a, right_b = refs[4 * job : 4 * job + 4]

        @pl.when(pl.program_id(0) == job)
        def _():
            total = dot(left_a[...], right_a[...], TN) + dot(left_b[...], right_b[...], TN)
            out_ref[...] = total.astype(BF16)


def weight_grad(*jobs):
    tokens, rows = jobs[0][0][0].shape
    width = jobs[0][1][0].shape[1]
    tile = min(512, rows)
    steps = rows // tile

    def left_spec(job):
        def index(j, i):
            return 0, jnp.where(j == job, i, jnp.where(j < job, 0, steps - 1))

        return pl.BlockSpec((tokens, tile), index)

    in_specs, operands = [], []
    for job, (lefts, rights) in enumerate(jobs):
        in_specs += [left_spec(job)] * 2
        in_specs += [pl.BlockSpec((tokens, width), lambda j, i: (0, 0))] * 2
        operands += list(lefts) + list(rights)
    return pl.pallas_call(
        functools.partial(weight_grad_kernel, len(jobs)),
        grid=(len(jobs), steps),
        in_specs=in_specs,
        out_specs=pl.BlockSpec((tile, width), lambda j, i: (i, j)),
        out_shape=jax.ShapeDtypeStruct((rows, len(jobs) * width), BF16),
        compiler_params=params("arbitrary", "arbitrary"),
        cost_estimate=SMALL_COST,
        name="weight_grad",
    )(*operands)


def mlp_kernel(
    xa_ref, xb_ref, ga_ref, gb_ref, mod_ref, up_ref, down_ref, bias_ref,
    x_out, g_out, hid_ref, gpre_ref, near_ref, far_ref, gnear_ref, gfar_ref, gbias_ref, gate_ref,
):
    x = pick(xa_ref, xb_ref)
    grad = (pick(ga_ref, gb_ref).astype(F32) * row(mod_ref, 5)).astype(BF16)
    x_out[...] = x
    g_out[...] = grad
    pre = dot(x, up_ref[...]) + bias_ref[...].astype(F32)
    square = pre * pre
    th = jnp.tanh(pre * (GELU_C + (GELU_C * GELU_A) * square))
    half = 0.5 + 0.5 * th
    hidden = (pre * half).astype(BF16)
    slope = half + pre * (1.0 - th * th) * (0.5 * GELU_C + (1.5 * GELU_A * GELU_C) * square)
    g_pre = (dot(grad, down_ref[...]) * slope).astype(BF16)
    hid_ref[...] = hidden
    gpre_ref[...] = g_pre
    put(gnear_ref, gfar_ref, dot(g_pre, up_ref[...], NT).astype(BF16))
    branch = dot(hidden, down_ref[...], NT)
    put(near_ref, far_ref, branch.astype(BF16))
    add_sums(gbias_ref, [g_pre.astype(F32)])
    add_sums(gate_ref, [branch * pick(ga_ref, gb_ref).astype(F32)])


def mlp(x_pieces, g_pieces, mod, weights, bias):
    count, width = x_pieces[0].shape
    tokens, tile = 2 * count, count // HALF_STEPS
    hidden = bias.shape[1]
    rows = lambda cols: pl.BlockSpec((tile, cols), lambda i: (i, 0))
    whole = lambda r, c: pl.BlockSpec((r, c), lambda i: (0, 0))
    return pl.pallas_call(
        mlp_kernel,
        grid=(2 * HALF_STEPS,),
        in_specs=two_parts(tile, width)
        + two_parts(tile, width)
        + [
            whole(*mod.shape),
            pl.BlockSpec((width, hidden), lambda i: (0, 0)),
            pl.BlockSpec((width, hidden), lambda i: (0, 1)),
            whole(1, hidden),
        ],
        out_specs=[rows(width), rows(width), rows(hidden), rows(hidden)]
        + two_parts(tile, width)
        + two_parts(tile, width)
        + [whole(8, hidden), whole(8, width)],
        out_shape=[
            jax.ShapeDtypeStruct((tokens, width), BF16),
            jax.ShapeDtypeStruct((tokens, width), BF16),
            jax.ShapeDtypeStruct((tokens, hidden), BF16),
            jax.ShapeDtypeStruct((tokens, hidden), BF16),
        ]
        + [jax.ShapeDtypeStruct((count, width), BF16)] * 4
        + [jax.ShapeDtypeStruct((8, hidden), F32), jax.ShapeDtypeStruct((8, width), F32)],
        compiler_params=params("arbitrary"),
        cost_estimate=SMALL_COST,
        name="feed_forward",
    )(*x_pieces, *g_pieces, mod, weights, weights, bias)


def attn_grad_kernel(xa, xb, qa, qb, ga, gb, va, vb, out_ref):
    wide = qa.shape[1]
    first = dot(xa[...], qa[...], TN) + dot(xb[...], qb[...], TN)
    out_ref[:, :wide] = first.astype(BF16)
    second = dot(ga[...], va[...], TN) + dot(gb[...], vb[...], TN)
    out_ref[:, wide:] = second.astype(BF16)


def attn_grad(*operands):
    tokens, rows = operands[0].shape
    wide, narrow = operands[2].shape[1], operands[6].shape[1]
    tile = min(256, rows)
    left = pl.BlockSpec((tokens, tile), lambda i: (0, i))
    right = lambda width: pl.BlockSpec((tokens, width), lambda i: (0, 0))
    return pl.pallas_call(
        attn_grad_kernel,
        grid=(rows // tile,),
        in_specs=[left, left, right(wide), right(wide), left, left, right(narrow), right(narrow)],
        out_specs=pl.BlockSpec((tile, wide + narrow), lambda i: (i, 0)),
        out_shape=jax.ShapeDtypeStruct((rows, wide + narrow), BF16),
        compiler_params=params("arbitrary"),
        cost_estimate=SMALL_COST,
        name="attn_grad",
    )(*operands)


def swap(value, bit):
    n = lax.axis_size("tensor")
    return lax.ppermute(value, "tensor", [(i, i ^ bit) for i in range(n)])


def joined(*values):
    return lax.optimization_barrier(values)


def after(value, token):
    return lax.optimization_barrier((value, token))[0]


def with_core(near, core):
    count = near.shape[0] // 2
    return (near[count:].astype(F32) + core[count:].astype(F32)).astype(BF16)


def halve(value, bit):
    n = lax.axis_size("dp")
    count, rows, width = value.shape
    mine = (lax.axis_index("dp") // bit) % 2
    value = value.reshape(count // 2, 2, rows, width)
    keep = lax.dynamic_index_in_dim(value, mine, 1, keepdims=False)
    send = lax.dynamic_index_in_dim(value, 1 - mine, 1, keepdims=False)
    return keep, lax.ppermute(send, "dp", [(i, i ^ bit) for i in range(n)])


def summed(keep, received):
    return keep.astype(F32) + received.astype(F32)


def exchange(value):
    return lax.all_to_all(value, "dp", 0, 0, tiled=True).reshape(value.shape)


def per_device(
    latents,
    conditioning,
    mod_weight,
    mod_bias,
    qkv_weight,
    qkv_bias,
    proj_weight,
    proj_bias,
    expand_weight,
    expand_bias,
    reduce_weight,
    reduce_bias,
    out_grad,
):
    n_tensor = lax.axis_size("tensor")
    n_dp = lax.axis_size("dp")
    row_count, images, model_width = latents.shape
    local_width = qkv_weight.shape[2]
    hidden_width = expand_weight.shape[1]
    mod_rows = mod_weight.shape[0]
    both = range(images)

    attn_full = lax.all_gather(
        jnp.concatenate([qkv_weight.reshape(mod_rows, 3 * local_width), proj_weight], 1),
        "dp",
        axis=0,
        tiled=True,
    )
    qkv_full, proj_full = attn_full[:, : 3 * local_width], attn_full[:, 3 * local_width :]
    x = [latents[:, i] for i in both]
    grad_y = [out_grad[:, i] for i in both]
    recv_x0 = swap(x[0], 2)

    cond_float = conditioning.astype(F32)
    cond_low = jax.nn.silu(cond_float).astype(BF16)
    cond_cols = exchange(
        cond_low.reshape(images, n_dp, mod_rows).transpose(1, 0, 2)
    ).reshape(n_dp * images, mod_rows)
    mod_part = jnp.einsum("gd,dke->gke", cond_cols, mod_weight, preferred_element_type=F32)
    mod_part, recv_x0 = joined(mod_part, recv_x0)
    recv_x1 = swap(after(x[1], recv_x0), 2)
    mod_recv = exchange(mod_part.reshape(n_dp, images, 6, model_width))
    pair_x0 = jnp.concatenate([x[0], recv_x0])
    core_x0 = swap(pair_x0, 1)
    mod_recv, core_x0, recv_x1 = joined(mod_recv, core_x0, recv_x1)
    recv_g = swap(after(out_grad, recv_x1), 2)
    pair_x = [pair_x0, jnp.concatenate([x[1], recv_x1])]
    core_x1 = swap(pair_x[1], 1)
    modulation = jnp.sum(mod_recv, 0) + mod_bias.astype(F32)[None]
    mod = [modulation[i] for i in both]

    ff_full = lax.all_gather(
        after(jnp.concatenate([expand_weight, reduce_weight], 1), modulation),
        "dp",
        axis=0,
        tiled=True,
    )

    bias_qkv = qkv_bias.reshape(1, 3 * local_width)
    bias_row = proj_bias.reshape(1, model_width)
    bias_out = reduce_bias.reshape(1, model_width)
    bias_hidden = expand_bias.reshape(1, hidden_width)

    def middle(i, pieces):
        return by_rows(
            middle_kernel,
            "middle",
            list(pieces) + [x[i]],
            [mod[i], bias_row],
            [F32, F32, BF16],
            False,
        )

    sh0, qkv0 = norm_project((pair_x[0], core_x0), mod[0], attn_full, bias_qkv)
    att0, lse0 = attend(qkv0)
    att0, recv_g, core_x1 = joined(att0, recv_g, core_x1)
    near0, far0 = project(att0, proj_full)
    core0 = swap(far0, 1)
    sh1, qkv1 = norm_project((after(pair_x[1], near0), core_x1), mod[1], attn_full, bias_qkv)
    qkv1, core0 = joined(qkv1, core0)
    chip0 = with_core(near0, core0)
    recv0 = swap(chip0, 2)
    pair_g = [jnp.concatenate([grad_y[i], recv_g[:, i]]) for i in both]
    core_g = [swap(v, 1) for v in pair_g]
    att1, lse1 = attend(after(qkv1, (chip0, pair_g)))
    att1, recv0, core_g = joined(att1, recv0, core_g)
    branch0, mid0, low0 = middle(0, (near0, core0, recv0))
    recv_m0 = swap(low0, 2)
    near1, far1 = project(after(att1, low0), proj_full)
    core1 = swap(far1, 1)
    recv1 = swap(with_core(near1, core1), 2)
    recv1, recv_m0 = joined(recv1, recv_m0)
    pair_m0 = jnp.concatenate([low0, recv_m0])
    core_m0 = swap(pair_m0, 1)
    branch1, mid1, low1 = middle(1, (near1, core1, recv1))
    low1, core_m0 = joined(low1, core_m0)
    recv_m1 = swap(low1, 2)
    shifted_a, attended, lse = [sh0, sh1], [att0, att1], [lse0, lse1]
    branch_a, mid = [branch0, branch1], [mid0, mid1]

    def feed(i, pieces):
        return mlp(pieces, (pair_g[i], core_g[i]), mod[i], ff_full, bias_hidden)

    ff0 = feed(0, (after(pair_m0, low1), core_m0))
    ff0, recv_m1 = joined(ff0, recv_m1)
    core0 = swap(ff0[7], 1)
    pair_m1 = jnp.concatenate([low1, recv_m1])
    core_m1 = swap(pair_m1, 1)
    chip0 = with_core(ff0[6], core0)
    recv0 = swap(chip0, 2)
    ff1 = feed(1, after((pair_m1, core_m1), chip0))
    ff1, recv0 = joined(ff1, recv0)
    ff = [ff0, ff1]
    own_g = [v.astype(F32) for v in grad_y]
    gate_m = [
        ff[i][9][:1] + bias_out.astype(F32) * jnp.sum(own_g[i], 0, keepdims=True) for i in both
    ]
    g_reduce_own = sum(
        jnp.sum((own_g[i] * mod[i][5:6]).astype(BF16).astype(F32), 0, keepdims=True) for i in both
    )

    def middle_back(i, pieces):
        return by_rows(
            middle_back_kernel,
            "middle_back",
            list(pieces) + [mid[i], grad_y[i], branch_a[i]],
            [mod[i]],
            [F32, BF16],
            True,
        )

    core1 = swap(ff1[7], 1)
    gmid0, ga0, sums_m0 = middle_back(0, (ff0[6], core0, recv0))
    ga0, core1 = joined(ga0, core1)
    recv_ga0 = swap(ga0, 2)
    chip1 = with_core(ff1[6], core1)
    recv1 = swap(chip1, 2)
    core_b = [swap(after(f[5], ga0), 1) for f in ff]
    x_parts, g_parts = after(([f[0] for f in ff], [f[1] for f in ff]), (ga0, chip1))
    g_ff = weight_grad((x_parts, [f[3] for f in ff]), (g_parts, [f[2] for f in ff]))
    g_ff, recv_ga0, recv1, core_b = joined(g_ff, recv_ga0, recv1, core_b)
    g_ff_w = lax.psum_scatter(g_ff, "dp", scatter_dimension=0, tiled=True)
    pair_ga0 = jnp.concatenate([ga0, recv_ga0])
    core_ga0 = swap(pair_ga0, 1)
    gmid1, ga1, sums_m1 = middle_back(1, (ff1[6], core1, recv1))
    ga1, core_ga0 = joined(ga1, core_ga0)
    recv_ga1 = swap(ga1, 2)
    full_ga0 = jnp.concatenate([after(pair_ga0, ga1), core_ga0])
    grad_mid, grad_a, sums_m = [gmid0, gmid1], [ga0, ga1], [sums_m0, sums_m1]

    def finish(i, pieces):
        return by_rows(
            result_kernel,
            "result",
            list(pieces) + [mid[i]],
            [mod[i], bias_out],
            [BF16],
            False,
        )[0]

    gatt0 = dot(full_ga0, proj_full).astype(BF16)
    gqkv0 = attend_back(qkv0, gatt0, lse0)
    gqkv0, recv_ga1 = joined(gqkv0, recv_ga1)
    pair_ga1 = jnp.concatenate([ga1, recv_ga1])
    core_ga1 = swap(pair_ga1, 1)
    near0, far0 = project(gqkv0, qkv_full)
    near0, far0, core_ga1 = joined(near0, far0, core_ga1)
    core0 = swap(far0, 1)
    full_ga = [full_ga0, jnp.concatenate([pair_ga1, core_ga1])]
    gatt1 = dot(after(full_ga[1], far0), proj_full).astype(BF16)
    gatt1, core0 = joined(gatt1, core0)
    chip0 = with_core(near0, core0)
    recv0 = swap(chip0, 2)
    gqkv1 = attend_back(qkv1, after(gatt1, chip0), lse1)
    gqkv1, recv0 = joined(gqkv1, recv0)
    grad_qkv = [gqkv0, gqkv1]
    g_attn = attn_grad(*shifted_a, *grad_qkv, *full_ga, *attended)
    keep, received = halve(g_attn.reshape(n_dp, mod_rows, -1), 1)
    near1, far1 = project(after(gqkv1, keep), qkv_full)
    core1 = swap(far1, 1)
    sums_p1 = row_sums((near1, far1), (pair_x[1], core_x1))
    sums_p1, core1 = joined(sums_p1, core1)

    def last(i, pieces):
        return by_rows(
            last_kernel, "last", list(pieces) + [x[i], grad_mid[i]], [mod[i]], [F32], True
        )

    lat0, sums_a0 = last(0, (near0, core0, after(recv0, sums_p1)))
    sums_a = [sums_a0, sums_p1]

    shared = jnp.concatenate(
        [jnp.concatenate([sums_a[i][:2], sums_m[i][2:3], sums_m[i][:2], gate_m[i]]) for i in both]
        + [sum(s[3:4] for s in sums_m), g_reduce_own]
    )
    shared, received = joined(shared, received)
    keep, received = halve(summed(keep, received).astype(BF16), 2)
    shared = shared + swap(after(shared, keep), 1)
    chip1 = with_core(near1, core1)
    recv1 = swap(after(chip1, shared), 2)
    recv_b = [swap(after(with_core(ff[i][4], core_b[i]), chip1), 2) for i in both]
    shared = shared + swap(shared, 2)
    local = jnp.concatenate(
        [
            sum(jnp.sum(v.astype(F32), 0) for v in grad_qkv),
            sum(f[8][0] for f in ff),
        ]
    )
    n_mod = images * 6 * model_width
    shared = shared.reshape(-1)
    local = jnp.concatenate([shared[n_mod:], local])
    high = local.astype(BF16)
    mine = jnp.concatenate(
        [shared[:n_mod].astype(BF16), high, (local - high.astype(F32)).astype(BF16)]
    )
    everyone = exchange(jnp.broadcast_to(mine[None], (n_dp,) + mine.shape))
    everyone, received, g_ff_w = joined(everyone, received, g_ff_w)
    everyone = everyone.astype(F32)
    keep, received = halve(summed(keep, received).astype(BF16), 4)
    lat1 = last(1, (near1, core1, recv1))[0]
    grad_latent = [lat0, lat1]
    g_mod_all = everyone[:, :n_mod].reshape(n_dp * images, 6, model_width)
    biases = jnp.sum(everyone[:, n_mod:].reshape(n_dp, 2, -1), (0, 1))
    sizes = [model_width, model_width, 3 * local_width, hidden_width]
    cuts = [sum(sizes[:n]) for n in range(len(sizes) + 1)]
    g_proj_b, g_reduce_b, g_qkv_b, g_expand_b = (
        biases[lo:hi] for lo, hi in zip(cuts, cuts[1:])
    )

    g_mod_b = jnp.sum(g_mod_all, 0)
    g_mod_low = g_mod_all.astype(BF16)
    mod_cols = model_width // n_tensor
    own_cols = lax.dynamic_slice_in_dim(
        g_mod_low, lax.axis_index("tensor") * mod_cols, mod_cols, 2
    )
    g_mod_w = jnp.einsum("gd,gke->dke", cond_cols, own_cols, preferred_element_type=F32)
    act_rows = jnp.einsum("gke,dke->gd", g_mod_low, mod_weight, preferred_element_type=F32)
    act_rows, keep = joined(act_rows, keep)
    result = [finish(i, (ff[i][4], core_b[i], after(recv_b[i], act_rows))) for i in both]
    grad_act = (
        exchange(act_rows.reshape(n_dp, images, mod_rows))
        .transpose(1, 0, 2)
        .reshape(images, n_dp * mod_rows)
    )
    silu_out, silu_pull = jax.vjp(jax.nn.silu, cond_float)
    grad_cond = silu_pull(grad_act)[0]
    received, g_ff_w = after((received, g_ff_w), (grad_cond, result, grad_latent))
    g_attn_w = summed(keep, received)
    bit = 8
    while bit < n_dp:
        g_attn_w = summed(*halve(g_attn_w.astype(BF16), bit))
        bit *= 2
    g_attn_w = g_attn_w[0]
    g_expand_w = g_ff_w[:, :hidden_width].astype(F32)
    g_reduce_w = g_ff_w[:, hidden_width:].astype(F32)
    g_qkv_w = g_attn_w[:, : 3 * local_width].reshape(mod_rows, 3, local_width)
    g_proj_w = g_attn_w[:, 3 * local_width :]
    return (
        jnp.stack(result, 1),
        jnp.stack(grad_latent, 1),
        grad_cond,
        g_mod_w,
        g_mod_b,
        g_qkv_w,
        g_qkv_b.reshape(3, local_width),
        g_proj_w,
        g_proj_b,
        g_expand_w,
        g_expand_b,
        g_reduce_w,
        g_reduce_b,
    )


def solution(mesh):
    in_specs = (
        P("tensor", "dp", None),
        P("dp", None),
        P("dp", None, None),
        P(),
        P("dp", None, "tensor"),
        P(None, "tensor"),
        P("dp", "tensor"),
        P(),
        P("dp", "tensor"),
        P("tensor"),
        P("dp", "tensor"),
        P(),
        P("tensor", "dp", None),
    )
    out_specs = (
        P("tensor", "dp", None),
        P("tensor", "dp", None),
        P("dp", None),
        P("dp", None, "tensor"),
        P(),
        P("dp", None, "tensor"),
        P(None, "tensor"),
        P("dp", "tensor"),
        P(),
        P("dp", "tensor"),
        P("tensor"),
        P("dp", "tensor"),
        P(),
    )
    return jax.shard_map(
        per_device, mesh=mesh, in_specs=in_specs, out_specs=out_specs, check_vma=False
    )
```

```python
import functools

import jax
import jax.numpy as jnp
from jax import lax
from jax.experimental import pallas as pl
from jax.experimental.pallas import tpu as pltpu
from jax.sharding import PartitionSpec as P

HEAD_DIM = 64
F32 = jnp.float32
BF16 = jnp.bfloat16
LOG2E = 1.4426950408889634
GELU_C = 0.7978845608028654
GELU_A = 0.044715
NN = (((1,), (0,)), ((), ()))
NT = (((1,), (1,)), ((), ()))
TN = (((0,), (0,)), ((), ()))
SMALL_COST = pl.CostEstimate(flops=1000, bytes_accessed=1000, transcendentals=0)
HALF_STEPS = 2
VMEM_BYTES = 56 * 1024 * 1024


def dot(left, right, dims=NN):
    return lax.dot_general(left, right, dims, preferred_element_type=F32)


def params(*kinds):
    return pltpu.CompilerParams(dimension_semantics=kinds, vmem_limit_bytes=VMEM_BYTES)


def attend_kernel(chunk, q_ref, k_ref, v_ref, out_ref, lse_ref):
    length, width = q_ref.shape
    factor = HEAD_DIM ** (-0.5) * LOG2E
    values_t = v_ref[...].astype(F32).T.astype(BF16)
    keys = [k_ref[:, lo : lo + HEAD_DIM] for lo in range(0, width, HEAD_DIM)]

    def body(step, carry):
        rows = pl.ds(pl.multiple_of(step * chunk, chunk), chunk)
        outs = []
        for head, key in enumerate(keys):
            lo = head * HEAD_DIM
            scores = dot(key, q_ref[rows, lo : lo + HEAD_DIM], NT)
            top = jnp.max(scores, 0, keepdims=True)
            weights = jnp.exp2((scores - top) * factor)
            total = jnp.sum(weights, 0, keepdims=True)
            out_t = dot(values_t[lo : lo + HEAD_DIM], weights.astype(BF16))
            outs.append(out_t / total)
            lse_ref[0, head : head + 1, rows] = top * factor + jnp.log(total) * LOG2E
        out_ref[rows, :] = jnp.concatenate(outs, 0).T.astype(BF16)
        return carry

    lax.fori_loop(0, length // chunk, body, 0, unroll=True)


def attend(qkv):
    length, three = qkv.shape
    width = three // 3
    pairs = width // 128
    chunk = min(1024, length)
    spec = lambda part: pl.BlockSpec((length, 128), lambda i: (0, part * pairs + i))
    return pl.pallas_call(
        functools.partial(attend_kernel, chunk),
        grid=(pairs,),
        in_specs=[spec(0), spec(1), spec(2)],
        out_specs=[
            pl.BlockSpec((length, 128), lambda i: (0, i)),
            pl.BlockSpec((1, 8, length), lambda i: (i, 0, 0)),
        ],
        out_shape=[
            jax.ShapeDtypeStruct((length, width), BF16),
            jax.ShapeDtypeStruct((pairs, 8, length), F32),
        ],
        compiler_params=params("arbitrary"),
        cost_estimate=SMALL_COST,
        name="attend",
    )(qkv, qkv, qkv)


def attend_back_kernel(chunk, q_ref, k_ref, v_ref, g_ref, lse_ref, out_ref, dk_ref, dv_ref):
    length, width = q_ref.shape
    total_width = out_ref.shape[1] // 3
    scale = HEAD_DIM ** (-0.5)
    factor = scale * LOG2E
    pair = pl.program_id(0)
    keys_t = k_ref[...].astype(F32).T.astype(BF16)
    heads = range(0, width, HEAD_DIM)
    keys = [k_ref[:, lo : lo + HEAD_DIM] for lo in heads]
    values = [v_ref[:, lo : lo + HEAD_DIM] for lo in heads]
    dk_ref[...] = jnp.zeros_like(dk_ref)
    dv_ref[...] = jnp.zeros_like(dv_ref)

    def columns(part):
        return pl.ds(pl.multiple_of(part * total_width + pair * width, width), width)

    def body(step, carry):
        rows = pl.ds(pl.multiple_of(step * chunk, chunk), chunk)
        outs = []
        for head, (key, value) in enumerate(zip(keys, values)):
            lo = head * HEAD_DIM
            query = q_ref[rows, lo : lo + HEAD_DIM]
            grad = g_ref[rows, lo : lo + HEAD_DIM]
            probs = jnp.exp2(dot(key, query, NT) * factor - lse_ref[0, head : head + 1, rows])
            dv_ref[head] += dot(probs.astype(BF16), grad)
            weighted = probs * dot(value, grad, NT)
            row_dot = jnp.sum(weighted, 0, keepdims=True)
            g_scores = (weighted - probs * row_dot).astype(BF16)
            dk_ref[head] += dot(g_scores, query)
            outs.append(dot(keys_t[lo : lo + HEAD_DIM], g_scores) * scale)
        out_ref[rows, columns(0)] = jnp.concatenate(outs, 0).T.astype(BF16)
        return carry

    lax.fori_loop(0, length // chunk, body, 0, unroll=True)
    n_heads = len(keys)
    out_ref[:, columns(1)] = (
        jnp.concatenate([dk_ref[h] for h in range(n_heads)], 1) * scale
    ).astype(BF16)
    out_ref[:, columns(2)] = jnp.concatenate([dv_ref[h] for h in range(n_heads)], 1).astype(BF16)


def attend_back(qkv, grad_att, lse):
    length, three = qkv.shape
    width = three // 3
    pairs = width // 128
    chunk = min(1024, length)
    spec = lambda part: pl.BlockSpec((length, 128), lambda i: (0, part * pairs + i))
    return pl.pallas_call(
        functools.partial(attend_back_kernel, chunk),
        grid=(pairs,),
        in_specs=[
            spec(0),
            spec(1),
            spec(2),
            pl.BlockSpec((length, 128), lambda i: (0, i)),
            pl.BlockSpec((1, 8, length), lambda i: (i, 0, 0)),
        ],
        out_specs=pl.BlockSpec((length, three), lambda i: (0, 0)),
        out_shape=jax.ShapeDtypeStruct((length, three), BF16),
        scratch_shapes=[
            pltpu.VMEM((128 // HEAD_DIM, length, HEAD_DIM), F32),
            pltpu.VMEM((128 // HEAD_DIM, length, HEAD_DIM), F32),
        ],
        compiler_params=params("arbitrary"),
        cost_estimate=SMALL_COST,
        name="attend_back",
    )(qkv, qkv, qkv, grad_att, lse)


def norm_parts(values):
    centered = values - jnp.mean(values, -1, keepdims=True)
    scale = lax.rsqrt(jnp.mean(centered * centered, -1, keepdims=True) + 1e-06)
    return centered * scale, scale


def norm_back(normed, scale, grad):
    mean_g = jnp.mean(grad, -1, keepdims=True)
    mean_gn = jnp.mean(grad * normed, -1, keepdims=True)
    return scale * (grad - mean_g - normed * mean_gn)


def row(ref, index):
    return ref[index : index + 1, :]


def add_sums(ref, values):
    @pl.when(pl.program_id(0) == 0)
    def _():
        ref[...] = jnp.zeros_like(ref)

    for index, value in enumerate(values):
        ref[index : index + 1, :] += jnp.sum(value, 0, keepdims=True)


def total_of(near_ref, core_ref, chip_ref):
    near = near_ref[...].astype(F32) + core_ref[...].astype(F32)
    return near + chip_ref[...].astype(F32)


def middle_kernel(near, core, chip, x_ref, mod_ref, bias_ref, branch_ref, mid_ref, out_ref):
    branch = total_of(near, core, chip) + bias_ref[...].astype(F32)
    mid = x_ref[...].astype(F32) + row(mod_ref, 2) * branch
    normed, _ = norm_parts(mid)
    branch_ref[...] = branch
    mid_ref[...] = mid
    out_ref[...] = (normed * (1.0 + row(mod_ref, 4)) + row(mod_ref, 3)).astype(BF16)


def middle_back_kernel(
    near, core, chip, mid_ref, g_ref, branch_ref, mod_ref, gmid_ref, ga_ref, sums_ref
):
    g_sm = total_of(near, core, chip)
    normed, scale = norm_parts(mid_ref[...])
    g_mid = g_ref[...].astype(F32) + norm_back(normed, scale, g_sm * (1.0 + row(mod_ref, 4)))
    g_a = (g_mid * row(mod_ref, 2)).astype(BF16)
    gmid_ref[...] = g_mid
    ga_ref[...] = g_a
    add_sums(sums_ref, [g_sm, g_sm * normed, g_mid * branch_ref[...], g_a.astype(F32)])


def last_kernel(near, core, chip, x_ref, gmid_ref, mod_ref, out_ref, sums_ref):
    g_sa = total_of(near, core, chip)
    normed, scale = norm_parts(x_ref[...].astype(F32))
    out_ref[...] = gmid_ref[...] + norm_back(normed, scale, g_sa * (1.0 + row(mod_ref, 1)))
    add_sums(sums_ref, [g_sa, g_sa * normed])


def result_kernel(near, core, chip, mid_ref, mod_ref, bias_ref, out_ref):
    branch = total_of(near, core, chip) + bias_ref[...].astype(F32)
    out_ref[...] = (mid_ref[...] + row(mod_ref, 5) * branch).astype(BF16)


def by_rows(kernel, name, tall, wide, outs, sums):
    count, width = tall[-1].shape
    tile = min(128, count)
    tiled = pl.BlockSpec((tile, width), lambda i: (i, 0))
    out_specs = [tiled] * len(outs)
    out_shape = [jax.ShapeDtypeStruct((count, width), t) for t in outs]
    if sums:
        out_specs.append(pl.BlockSpec((8, width), lambda i: (0, 0)))
        out_shape.append(jax.ShapeDtypeStruct((8, width), F32))
    return pl.pallas_call(
        kernel,
        grid=(count // tile,),
        in_specs=[tiled] * len(tall) + [pl.BlockSpec(w.shape, lambda i: (0, 0)) for w in wide],
        out_specs=out_specs,
        out_shape=out_shape,
        compiler_params=params("arbitrary"),
        cost_estimate=SMALL_COST,
        name=name,
    )(*tall, *wide)


def two_parts(tile, width):
    return [
        pl.BlockSpec((tile, width), lambda i: (jnp.minimum(i, HALF_STEPS - 1), 0)),
        pl.BlockSpec((tile, width), lambda i: (jnp.maximum(i - HALF_STEPS, 0), 0)),
    ]


def pick(first_ref, second_ref):
    return jnp.where(pl.program_id(0) < HALF_STEPS, first_ref[...], second_ref[...])


def put(first_ref, second_ref, value):
    @pl.when(pl.program_id(0) < HALF_STEPS)
    def _():
        first_ref[...] = value

    @pl.when(pl.program_id(0) >= HALF_STEPS)
    def _():
        second_ref[...] = value


def norm_project_kernel(xa_ref, xb_ref, mod_ref, w_ref, bias_ref, shifted_ref, out_ref):
    normed, _ = norm_parts(pick(xa_ref, xb_ref).astype(F32))
    shifted = (normed * (1.0 + row(mod_ref, 1)) + row(mod_ref, 0)).astype(BF16)
    shifted_ref[...] = shifted
    out_ref[...] = (dot(shifted, w_ref[...]) + bias_ref[...].astype(F32)).astype(BF16)


def norm_project(pieces, mod, weight, bias):
    count, width = pieces[0].shape
    tokens, tile = 2 * count, count // HALF_STEPS
    outs = bias.shape[1]
    whole = lambda r, c: pl.BlockSpec((r, c), lambda i: (0, 0))
    return pl.pallas_call(
        norm_project_kernel,
        grid=(2 * HALF_STEPS,),
        in_specs=two_parts(tile, width) + [whole(*mod.shape), whole(width, outs), whole(1, outs)],
        out_specs=[pl.BlockSpec((tile, c), lambda i: (i, 0)) for c in (width, outs)],
        out_shape=[jax.ShapeDtypeStruct((tokens, c), BF16) for c in (width, outs)],
        compiler_params=params("arbitrary"),
        cost_estimate=SMALL_COST,
        name="norm_project",
    )(*pieces, mod, weight, bias)


def row_sums_kernel(pa_ref, pb_ref, xa_ref, xb_ref, sums_ref):
    part = pick(pa_ref, pb_ref).astype(F32)
    normed, _ = norm_parts(pick(xa_ref, xb_ref).astype(F32))
    add_sums(sums_ref, [part, part * normed])


def row_sums(parts, rows):
    count, width = parts[0].shape
    tile = count // HALF_STEPS
    return pl.pallas_call(
        row_sums_kernel,
        grid=(2 * HALF_STEPS,),
        in_specs=two_parts(tile, width) + two_parts(tile, width),
        out_specs=pl.BlockSpec((8, width), lambda i: (0, 0)),
        out_shape=jax.ShapeDtypeStruct((8, width), F32),
        compiler_params=params("arbitrary"),
        cost_estimate=SMALL_COST,
        name="row_sums",
    )(*parts, *rows)


def project(x, weight):
    half = x.shape[0] // 2
    far = dot(x[half:], weight, NT).astype(BF16)
    return dot(x[:half], weight, NT).astype(BF16), far


def weight_grad_kernel(n_jobs, *refs):
    out_ref = refs[-1]
    for job in range(n_jobs):
        left_a, left_b, right_a, right_b = refs[4 * job : 4 * job + 4]

        @pl.when(pl.program_id(0) == job)
        def _():
            total = dot(left_a[...], right_a[...], TN) + dot(left_b[...], right_b[...], TN)
            out_ref[...] = total.astype(BF16)


def weight_grad(*jobs):
    tokens, rows = jobs[0][0][0].shape
    width = jobs[0][1][0].shape[1]
    tile = min(512, rows)
    steps = rows // tile

    def left_spec(job):
        def index(j, i):
            return 0, jnp.where(j == job, i, jnp.where(j < job, 0, steps - 1))

        return pl.BlockSpec((tokens, tile), index)

    in_specs, operands = [], []
    for job, (lefts, rights) in enumerate(jobs):
        in_specs += [left_spec(job)] * 2
        in_specs += [pl.BlockSpec((tokens, width), lambda j, i: (0, 0))] * 2
        operands += list(lefts) + list(rights)
    return pl.pallas_call(
        functools.partial(weight_grad_kernel, len(jobs)),
        grid=(len(jobs), steps),
        in_specs=in_specs,
        out_specs=pl.BlockSpec((tile, width), lambda j, i: (i, j)),
        out_shape=jax.ShapeDtypeStruct((rows, len(jobs) * width), BF16),
        compiler_params=params("arbitrary", "arbitrary"),
        cost_estimate=SMALL_COST,
        name="weight_grad",
    )(*operands)


def mlp_kernel(
    xa_ref, xb_ref, ga_ref, gb_ref, mod_ref, up_ref, down_ref, bias_ref,
    x_out, g_out, hid_ref, gpre_ref, near_ref, far_ref, gnear_ref, gfar_ref, gbias_ref, gate_ref,
):
    x = pick(xa_ref, xb_ref)
    grad = (pick(ga_ref, gb_ref).astype(F32) * row(mod_ref, 5)).astype(BF16)
    x_out[...] = x
    g_out[...] = grad
    pre = dot(x, up_ref[...]) + bias_ref[...].astype(F32)
    square = pre * pre
    th = jnp.tanh(pre * (GELU_C + (GELU_C * GELU_A) * square))
    half = 0.5 + 0.5 * th
    hidden = (pre * half).astype(BF16)
    slope = half + pre * (1.0 - th * th) * (0.5 * GELU_C + (1.5 * GELU_A * GELU_C) * square)
    g_pre = (dot(grad, down_ref[...]) * slope).astype(BF16)
    hid_ref[...] = hidden
    gpre_ref[...] = g_pre
    put(gnear_ref, gfar_ref, dot(g_pre, up_ref[...], NT).astype(BF16))
    branch = dot(hidden, down_ref[...], NT)
    put(near_ref, far_ref, branch.astype(BF16))
    add_sums(gbias_ref, [g_pre.astype(F32)])
    add_sums(gate_ref, [branch * pick(ga_ref, gb_ref).astype(F32)])


def mlp(x_pieces, g_pieces, mod, weights, bias):
    count, width = x_pieces[0].shape
    tokens, tile = 2 * count, count // HALF_STEPS
    hidden = bias.shape[1]
    rows = lambda cols: pl.BlockSpec((tile, cols), lambda i: (i, 0))
    whole = lambda r, c: pl.BlockSpec((r, c), lambda i: (0, 0))
    return pl.pallas_call(
        mlp_kernel,
        grid=(2 * HALF_STEPS,),
        in_specs=two_parts(tile, width)
        + two_parts(tile, width)
        + [
            whole(*mod.shape),
            pl.BlockSpec((width, hidden), lambda i: (0, 0)),
            pl.BlockSpec((width, hidden), lambda i: (0, 1)),
            whole(1, hidden),
        ],
        out_specs=[rows(width), rows(width), rows(hidden), rows(hidden)]
        + two_parts(tile, width)
        + two_parts(tile, width)
        + [whole(8, hidden), whole(8, width)],
        out_shape=[
            jax.ShapeDtypeStruct((tokens, width), BF16),
            jax.ShapeDtypeStruct((tokens, width), BF16),
            jax.ShapeDtypeStruct((tokens, hidden), BF16),
            jax.ShapeDtypeStruct((tokens, hidden), BF16),
        ]
        + [jax.ShapeDtypeStruct((count, width), BF16)] * 4
        + [jax.ShapeDtypeStruct((8, hidden), F32), jax.ShapeDtypeStruct((8, width), F32)],
        compiler_params=params("arbitrary"),
        cost_estimate=SMALL_COST,
        name="feed_forward",
    )(*x_pieces, *g_pieces, mod, weights, weights, bias)


def attn_grad_kernel(xa, xb, qa, qb, ga, gb, va, vb, out_ref):
    wide = qa.shape[1]
    first = dot(xa[...], qa[...], TN) + dot(xb[...], qb[...], TN)
    out_ref[:, :wide] = first.astype(BF16)
    second = dot(ga[...], va[...], TN) + dot(gb[...], vb[...], TN)
    out_ref[:, wide:] = second.astype(BF16)


def attn_grad(*operands):
    tokens, rows = operands[0].shape
    wide, narrow = operands[2].shape[1], operands[6].shape[1]
    tile = min(256, rows)
    left = pl.BlockSpec((tokens, tile), lambda i: (0, i))
    right = lambda width: pl.BlockSpec((tokens, width), lambda i: (0, 0))
    return pl.pallas_call(
        attn_grad_kernel,
        grid=(rows // tile,),
        in_specs=[left, left, right(wide), right(wide), left, left, right(narrow), right(narrow)],
        out_specs=pl.BlockSpec((tile, wide + narrow), lambda i: (i, 0)),
        out_shape=jax.ShapeDtypeStruct((rows, wide + narrow), BF16),
        compiler_params=params("arbitrary"),
        cost_estimate=SMALL_COST,
        name="attn_grad",
    )(*operands)


def swap(value, bit):
    n = lax.axis_size("tensor")
    return lax.ppermute(value, "tensor", [(i, i ^ bit) for i in range(n)])


def joined(*values):
    return lax.optimization_barrier(values)


def after(value, token):
    return lax.optimization_barrier((value, token))[0]


def with_core(near, core):
    count = near.shape[0] // 2
    return (near[count:].astype(F32) + core[count:].astype(F32)).astype(BF16)


def halve(value, bit):
    n = lax.axis_size("dp")
    count, rows, width = value.shape
    mine = (lax.axis_index("dp") // bit) % 2
    value = value.reshape(count // 2, 2, rows, width)
    keep = lax.dynamic_index_in_dim(value, mine, 1, keepdims=False)
    send = lax.dynamic_index_in_dim(value, 1 - mine, 1, keepdims=False)
    return keep, lax.ppermute(send, "dp", [(i, i ^ bit) for i in range(n)])


def summed(keep, received):
    return keep.astype(F32) + received.astype(F32)


def exchange(value):
    return lax.all_to_all(value, "dp", 0, 0, tiled=True).reshape(value.shape)


def per_device(
    latents,
    conditioning,
    mod_weight,
    mod_bias,
    qkv_weight,
    qkv_bias,
    proj_weight,
    proj_bias,
    expand_weight,
    expand_bias,
    reduce_weight,
    reduce_bias,
    out_grad,
):
    n_tensor = lax.axis_size("tensor")
    n_dp = lax.axis_size("dp")
    row_count, images, model_width = latents.shape
    local_width = qkv_weight.shape[2]
    hidden_width = expand_weight.shape[1]
    mod_rows = mod_weight.shape[0]
    both = range(images)

    attn_full = lax.all_gather(
        jnp.concatenate([qkv_weight.reshape(mod_rows, 3 * local_width), proj_weight], 1),
        "dp",
        axis=0,
        tiled=True,
    )
    qkv_full, proj_full = attn_full[:, : 3 * local_width], attn_full[:, 3 * local_width :]
    x = [latents[:, i] for i in both]
    grad_y = [out_grad[:, i] for i in both]
    recv_x0 = swap(x[0], 2)

    cond_float = conditioning.astype(F32)
    cond_low = jax.nn.silu(cond_float).astype(BF16)
    cond_cols = exchange(
        cond_low.reshape(images, n_dp, mod_rows).transpose(1, 0, 2)
    ).reshape(n_dp * images, mod_rows)
    mod_part = jnp.einsum("gd,dke->gke", cond_cols, mod_weight, preferred_element_type=F32)
    mod_part, recv_x0 = joined(mod_part, recv_x0)
    recv_x1 = swap(after(x[1], recv_x0), 2)
    mod_recv = exchange(mod_part.reshape(n_dp, images, 6, model_width))
    pair_x0 = jnp.concatenate([x[0], recv_x0])
    core_x0 = swap(pair_x0, 1)
    mod_recv, core_x0, recv_x1 = joined(mod_recv, core_x0, recv_x1)
    recv_g = swap(after(out_grad, recv_x1), 2)
    pair_x = [pair_x0, jnp.concatenate([x[1], recv_x1])]
    core_x1 = swap(pair_x[1], 1)
    modulation = jnp.sum(mod_recv, 0) + mod_bias.astype(F32)[None]
    mod = [modulation[i] for i in both]

    ff_full = lax.all_gather(
        after(jnp.concatenate([expand_weight, reduce_weight], 1), modulation),
        "dp",
        axis=0,
        tiled=True,
    )

    bias_qkv = qkv_bias.reshape(1, 3 * local_width)
    bias_row = proj_bias.reshape(1, model_width)
    bias_out = reduce_bias.reshape(1, model_width)
    bias_hidden = expand_bias.reshape(1, hidden_width)

    def middle(i, pieces):
        return by_rows(
            middle_kernel,
            "middle",
            list(pieces) + [x[i]],
            [mod[i], bias_row],
            [F32, F32, BF16],
            False,
        )

    sh0, qkv0 = norm_project((pair_x[0], core_x0), mod[0], attn_full, bias_qkv)
    att0, lse0 = attend(qkv0)
    att0, recv_g, core_x1 = joined(att0, recv_g, core_x1)
    near0, far0 = project(att0, proj_full)
    core0 = swap(far0, 1)
    sh1, qkv1 = norm_project((after(pair_x[1], near0), core_x1), mod[1], attn_full, bias_qkv)
    qkv1, core0 = joined(qkv1, core0)
    chip0 = with_core(near0, core0)
    recv0 = swap(chip0, 2)
    pair_g = [jnp.concatenate([grad_y[i], recv_g[:, i]]) for i in both]
    core_g = [swap(v, 1) for v in pair_g]
    att1, lse1 = attend(after(qkv1, (chip0, pair_g)))
    att1, recv0, core_g = joined(att1, recv0, core_g)
    branch0, mid0, low0 = middle(0, (near0, core0, recv0))
    recv_m0 = swap(low0, 2)
    near1, far1 = project(after(att1, low0), proj_full)
    core1 = swap(far1, 1)
    recv1 = swap(with_core(near1, core1), 2)
    recv1, recv_m0 = joined(recv1, recv_m0)
    pair_m0 = jnp.concatenate([low0, recv_m0])
    core_m0 = swap(pair_m0, 1)
    branch1, mid1, low1 = middle(1, (near1, core1, recv1))
    low1, core_m0 = joined(low1, core_m0)
    recv_m1 = swap(low1, 2)
    shifted_a, attended, lse = [sh0, sh1], [att0, att1], [lse0, lse1]
    branch_a, mid = [branch0, branch1], [mid0, mid1]

    def feed(i, pieces):
        return mlp(pieces, (pair_g[i], core_g[i]), mod[i], ff_full, bias_hidden)

    ff0 = feed(0, (after(pair_m0, low1), core_m0))
    ff0, recv_m1 = joined(ff0, recv_m1)
    core0 = swap(ff0[7], 1)
    pair_m1 = jnp.concatenate([low1, recv_m1])
    core_m1 = swap(pair_m1, 1)
    chip0 = with_core(ff0[6], core0)
    recv0 = swap(chip0, 2)
    ff1 = feed(1, after((pair_m1, core_m1), chip0))
    ff1, recv0 = joined(ff1, recv0)
    ff = [ff0, ff1]
    own_g = [v.astype(F32) for v in grad_y]
    gate_m = [
        ff[i][9][:1] + bias_out.astype(F32) * jnp.sum(own_g[i], 0, keepdims=True) for i in both
    ]
    g_reduce_own = sum(
        jnp.sum((own_g[i] * mod[i][5:6]).astype(BF16).astype(F32), 0, keepdims=True) for i in both
    )

    def middle_back(i, pieces):
        return by_rows(
            middle_back_kernel,
            "middle_back",
            list(pieces) + [mid[i], grad_y[i], branch_a[i]],
            [mod[i]],
            [F32, BF16],
            True,
        )

    core1 = swap(ff1[7], 1)
    gmid0, ga0, sums_m0 = middle_back(0, (ff0[6], core0, recv0))
    ga0, core1 = joined(ga0, core1)
    recv_ga0 = swap(ga0, 2)
    chip1 = with_core(ff1[6], core1)
    recv1 = swap(chip1, 2)
    core_b = [swap(after(f[5], ga0), 1) for f in ff]
    x_parts, g_parts = after(([f[0] for f in ff], [f[1] for f in ff]), (ga0, chip1))
    g_ff = weight_grad((x_parts, [f[3] for f in ff]), (g_parts, [f[2] for f in ff]))
    g_ff, recv_ga0, recv1, core_b = joined(g_ff, recv_ga0, recv1, core_b)
    g_ff_w = lax.psum_scatter(g_ff, "dp", scatter_dimension=0, tiled=True)
    pair_ga0 = jnp.concatenate([ga0, recv_ga0])
    core_ga0 = swap(pair_ga0, 1)
    gmid1, ga1, sums_m1 = middle_back(1, (ff1[6], core1, recv1))
    ga1, core_ga0 = joined(ga1, core_ga0)
    recv_ga1 = swap(ga1, 2)
    full_ga0 = jnp.concatenate([after(pair_ga0, ga1), core_ga0])
    grad_mid, grad_a, sums_m = [gmid0, gmid1], [ga0, ga1], [sums_m0, sums_m1]

    def finish(i, pieces):
        return by_rows(
            result_kernel,
            "result",
            list(pieces) + [mid[i]],
            [mod[i], bias_out],
            [BF16],
            False,
        )[0]

    gatt0 = dot(full_ga0, proj_full).astype(BF16)
    gqkv0 = attend_back(qkv0, gatt0, lse0)
    gqkv0, recv_ga1 = joined(gqkv0, recv_ga1)
    pair_ga1 = jnp.concatenate([ga1, recv_ga1])
    core_ga1 = swap(pair_ga1, 1)
    near0, far0 = project(gqkv0, qkv_full)
    near0, far0, core_ga1 = joined(near0, far0, core_ga1)
    core0 = swap(far0, 1)
    full_ga = [full_ga0, jnp.concatenate([pair_ga1, core_ga1])]
    gatt1 = dot(after(full_ga[1], far0), proj_full).astype(BF16)
    gatt1, core0 = joined(gatt1, core0)
    chip0 = with_core(near0, core0)
    recv0 = swap(chip0, 2)
    gqkv1 = attend_back(qkv1, after(gatt1, chip0), lse1)
    gqkv1, recv0 = joined(gqkv1, recv0)
    grad_qkv = [gqkv0, gqkv1]
    g_attn = attn_grad(*shifted_a, *grad_qkv, *full_ga, *attended)
    keep, received = halve(g_attn.reshape(n_dp, mod_rows, -1), 1)
    near1, far1 = project(after(gqkv1, keep), qkv_full)
    core1 = swap(far1, 1)
    sums_p1 = row_sums((near1, far1), (pair_x[1], core_x1))
    sums_p1, core1 = joined(sums_p1, core1)

    def last(i, pieces):
        return by_rows(
            last_kernel, "last", list(pieces) + [x[i], grad_mid[i]], [mod[i]], [F32], True
        )

    lat0, sums_a0 = last(0, (near0, core0, after(recv0, sums_p1)))
    sums_a = [sums_a0, sums_p1]

    shared = jnp.concatenate(
        [jnp.concatenate([sums_a[i][:2], sums_m[i][2:3], sums_m[i][:2], gate_m[i]]) for i in both]
        + [sum(s[3:4] for s in sums_m), g_reduce_own]
    )
    shared = shared + swap(shared, 1)
    chip1 = with_core(near1, core1)
    recv1 = swap(after(chip1, shared), 2)
    recv_b = [swap(after(with_core(ff[i][4], core_b[i]), chip1), 2) for i in both]
    shared = shared + swap(shared, 2)
    local = jnp.concatenate(
        [
            sum(jnp.sum(v.astype(F32), 0) for v in grad_qkv),
            sum(f[8][0] for f in ff),
        ]
    )
    n_mod = images * 6 * model_width
    shared = shared.reshape(-1)
    local = jnp.concatenate([shared[n_mod:], local])
    high = local.astype(BF16)
    mine = jnp.concatenate(
        [shared[:n_mod].astype(BF16), high, (local - high.astype(F32)).astype(BF16)]
    )
    everyone = exchange(jnp.broadcast_to(mine[None], (n_dp,) + mine.shape))
    everyone, received, g_ff_w = joined(everyone, received, g_ff_w)
    everyone = everyone.astype(F32)
    keep, received = halve(summed(keep, received).astype(BF16), 2)
    lat1 = last(1, (near1, core1, recv1))[0]
    grad_latent = [lat0, lat1]
    g_mod_all = everyone[:, :n_mod].reshape(n_dp * images, 6, model_width)
    biases = jnp.sum(everyone[:, n_mod:].reshape(n_dp, 2, -1), (0, 1))
    sizes = [model_width, model_width, 3 * local_width, hidden_width]
    cuts = [sum(sizes[:n]) for n in range(len(sizes) + 1)]
    g_proj_b, g_reduce_b, g_qkv_b, g_expand_b = (
        biases[lo:hi] for lo, hi in zip(cuts, cuts[1:])
    )

    g_mod_b = jnp.sum(g_mod_all, 0)
    g_mod_low = g_mod_all.astype(BF16)
    mod_cols = model_width // n_tensor
    own_cols = lax.dynamic_slice_in_dim(
        g_mod_low, lax.axis_index("tensor") * mod_cols, mod_cols, 2
    )
    g_mod_w = jnp.einsum("gd,gke->dke", cond_cols, own_cols, preferred_element_type=F32)
    act_rows = jnp.einsum("gke,dke->gd", g_mod_low, mod_weight, preferred_element_type=F32)
    act_rows, keep = joined(act_rows, keep)
    result = [finish(i, (ff[i][4], core_b[i], after(recv_b[i], act_rows))) for i in both]
    act_rows, received, result = joined(act_rows, received, result)
    keep, received = halve(summed(keep, received).astype(BF16), 4)
    grad_act = (
        exchange(act_rows.reshape(n_dp, images, mod_rows))
        .transpose(1, 0, 2)
        .reshape(images, n_dp * mod_rows)
    )
    silu_out, silu_pull = jax.vjp(jax.nn.silu, cond_float)
    grad_cond = silu_pull(grad_act)[0]
    received, g_ff_w = after((received, g_ff_w), (grad_cond, result, grad_latent))
    g_attn_w = summed(keep, received)
    bit = 8
    while bit < n_dp:
        g_attn_w = summed(*halve(g_attn_w.astype(BF16), bit))
        bit *= 2
    g_attn_w = g_attn_w[0]
    g_expand_w = g_ff_w[:, :hidden_width].astype(F32)
    g_reduce_w = g_ff_w[:, hidden_width:].astype(F32)
    g_qkv_w = g_attn_w[:, : 3 * local_width].reshape(mod_rows, 3, local_width)
    g_proj_w = g_attn_w[:, 3 * local_width :]
    return (
        jnp.stack(result, 1),
        jnp.stack(grad_latent, 1),
        grad_cond,
        g_mod_w,
        g_mod_b,
        g_qkv_w,
        g_qkv_b.reshape(3, local_width),
        g_proj_w,
        g_proj_b,
        g_expand_w,
        g_expand_b,
        g_reduce_w,
        g_reduce_b,
    )


def solution(mesh):
    in_specs = (
        P("tensor", "dp", None),
        P("dp", None),
        P("dp", None, None),
        P(),
        P("dp", None, "tensor"),
        P(None, "tensor"),
        P("dp", "tensor"),
        P(),
        P("dp", "tensor"),
        P("tensor"),
        P("dp", "tensor"),
        P(),
        P("tensor", "dp", None),
    )
    out_specs = (
        P("tensor", "dp", None),
        P("tensor", "dp", None),
        P("dp", None),
        P("dp", None, "tensor"),
        P(),
        P("dp", None, "tensor"),
        P(None, "tensor"),
        P("dp", "tensor"),
        P(),
        P("dp", "tensor"),
        P("tensor"),
        P("dp", "tensor"),
        P(),
    )
    return jax.shard_map(
        per_device, mesh=mesh, in_specs=in_specs, out_specs=out_specs, check_vma=False
    )
```
